32 devices in a mesh: cores: 4 (over y, core), samp: 8 (over z, x).
Axes of the slice: x: 2, y: 2, z: 4, core: 2. Of those that a mesh axis runs over, the one named last changes fastest.
Arguments:
- cores: float32 [4, 512, 2304], P('cores'), may hold values from -0.875 to 0.875
- indices: int32 [8192, 4], P('samp'), may hold values from 0 to 511
- observed: float32 [8192], P('samp'), may hold values from -6 to 6
- step_size: float32 [], replicated, may hold values from 0.2 to 0.6
Outputs:
- new_cores: float32 [4, 512, 2304], P('cores', 'samp')
The draws below stay inside these ranges and needn't reach their ends.
All inputs are finite; a program needn't handle non-finite values.
Results may differ from the reference program's by a relative error of at most 0.0003.
Values sent between devices are 32-bit elements; how exact they have to be, the bound alone decides.
A program may use at most 128 MiB of HBM per device.

```python
import math
import jax
import jax.numpy as jnp
from jax import lax

R = 48
N = 512
MODES = 4
SAMPLES = 8192


def draw_cores(key, part):
    factor_scale = R ** (-0.5)
    values = jax.random.normal(jax.random.fold_in(key, 13), (MODES, N, R * R), jnp.float32) * factor_scale
    return jnp.clip(values, -0.875, 0.875)


def with_ends(array, stream_key, smallest, high):
    index_at = [jax.random.randint(jax.random.fold_in(stream_key, axis), (), 0, length) for axis, length in enumerate(array.shape)]
    widest = array.shape.index(max(array.shape))
    next_to = index_at[:widest] + [(index_at[widest] + 1) % array.shape[widest]] + index_at[widest + 1:]
    return array.at[tuple(index_at)].set(smallest).at[tuple(next_to)].set(high)


def steps_of(rng, extent, shards, least, high):
    loudness, own = 1.0, jax.random.fold_in(rng, 6)
    for dim, parts in shards:
        heights = jnp.exp(jax.random.uniform(jax.random.fold_in(own, dim), (parts,), jnp.float32, least / len(shards), high / len(shards)))
        loudness = loudness * jnp.repeat(heights, extent[dim] // parts).reshape([-1 if axis == dim else 1 for axis in range(len(extent))])
    return loudness


def scatter_about(key, extent, width, bound, cuts=(), held_as=jnp.bfloat16):
    entries = jax.random.normal(key, extent, jnp.float32) * width
    if len(cuts) > 0:
        entries = steps_of(key, extent, cuts, -0.22, 0.18) * entries
    return jnp.clip(entries, min=-bound, max=bound).astype(held_as)


def setup_inputs(seed: int = 0) -> dict:
    streams_of = jax.random.split(jax.random.key(seed), 5)
    return {
        "cores": draw_cores(jax.random.fold_in(streams_of[4], 71), 0),
        "indices": with_ends(jax.random.randint(streams_of[1], (SAMPLES, MODES), 0, N), jax.random.fold_in(streams_of[1], 1), 0, N - 1).astype(jnp.int32),
        "observed": scatter_about(streams_of[2], (SAMPLES,), 1.0, 6.0, ((0, 8),), jnp.float32),
        "step_size": jnp.clip(jnp.exp(jax.random.uniform(streams_of[3], (), jnp.float32, math.log(0.2), math.log(0.6))), 0.2, 0.6),
    }


HIGH = lax.Precision.HIGHEST

def reference(cores, indices, observed, step_size):
    count = indices.shape[0]
    unit = (jnp.arange(R) == 0).astype(jnp.float32)
    mats = []
    for k in range(MODES):
        mats.append(jnp.take(cores[k], indices[:, k], axis=0).reshape(count, R, R))
    lefts = []
    vec = jnp.broadcast_to(unit, (count, R))
    for k in range(MODES):
        lefts.append(vec)
        vec = jnp.einsum('sa,sab->sb', vec, mats[k], precision=HIGH)
    rights = [None] * MODES
    vec = jnp.broadcast_to(unit, (count, R))
    for k in range(MODES - 1, -1, -1):
        rights[k] = vec
        vec = jnp.einsum('sab,sb->sa', mats[k], vec, precision=HIGH)
    mats = None
    predicted = jnp.sum(jnp.einsum('sa,sab->sb', lefts[0], jnp.take(cores[0], indices[:, 0], axis=0).reshape(count, R, R), precision=HIGH) * rights[0], axis=1)
    residual = predicted - observed
    carry = jnp.eye(R, dtype=jnp.float32)
    results = []
    for k in range(MODES):
        outer = (lefts[k][:, :, None] * (residual[:, None] * rights[k])[:, None, :]).reshape(count, R * R)
        gradient = jax.ops.segment_sum(outer, indices[:, k], num_segments=N)
        updated = (cores[k] - step_size * gradient).reshape(N, R, R)
        product = jnp.einsum('ac,icb->iab', carry, updated, precision=HIGH)
        if k < MODES - 1:
            gram = jnp.einsum('iab,iac->bc', product, product, precision=HIGH) / N
            lower = jnp.linalg.cholesky(gram)
            flat = product.reshape(N * R, R)
            ortho = lax.linalg.triangular_solve(lower, flat, left_side=False, lower=True, transpose_a=True)
            results.append(ortho.reshape(N, R * R))
            carry = lower.T
        else:
            results.append(product.reshape(N, R * R))
    return jnp.stack(results)
```

```python
import functools

import jax
import jax.numpy as jnp
from jax import lax
from jax.experimental import pallas as pl
from jax.experimental.pallas import tpu as pltpu
from jax.sharding import PartitionSpec as P

R = 48
N = 512
W = 64

HIGH = lax.Precision.HIGHEST
MESH = pl.DeviceIdType.MESH
F32 = jnp.float32
BF16 = jnp.bfloat16


def from_behind(array, axis, by):
    peers = lax.axis_size(axis)
    pairs = [(i, i + by) for i in range(peers) if 0 <= i + by < peers]
    return lax.ppermute(array, axis, pairs)


def split(x):
    high = x.astype(BF16)
    low = (x - high.astype(F32)).astype(BF16)
    return high, low


def stacked(mat):
    high, low = split(mat)
    return jnp.concatenate([high, high, low], axis=1)


def tall_of(wide, pairs):
    return jnp.concatenate([wide[:, 128 * p:128 * p + 128] for p in range(pairs)], axis=0)


def gram_kernel(ncores, nsamp, pairs, ustack, uth, utl, hprev, hown, sendbuf, got_prev, got_own,
                send_own, send_next, recv_own, recv_prev):
    mine = lax.axis_index("cores")
    me = lax.axis_index("samp")
    barrier = pltpu.get_barrier_semaphore()
    has_prev = mine > 0
    has_next = mine < ncores - 1

    def greet(mode, other):
        pl.semaphore_signal(barrier, inc=1, device_id=(mode, other), device_id_type=MESH)

    for d in range(1, nsamp):
        greet(mine, lax.rem(me + d, nsamp))

    @pl.when(has_prev)
    def _():
        for d in range(nsamp):
            greet(mine - 1, lax.rem(me + d, nsamp))

    pl.semaphore_wait(barrier, nsamp - 1 + nsamp * jnp.minimum(ncores - 1 - mine, 1))

    def own_copy(d):
        return pltpu.make_async_remote_copy(
            src_ref=sendbuf, dst_ref=got_own.at[d - 1], send_sem=send_own.at[d - 1],
            recv_sem=recv_own.at[d - 1], device_id=(mine, lax.rem(me + d, nsamp)), device_id_type=MESH)

    def next_copy(d):
        return pltpu.make_async_remote_copy(
            src_ref=sendbuf, dst_ref=got_prev.at[d], send_sem=send_next.at[d],
            recv_sem=recv_prev.at[d], device_id=(mine + 1, lax.rem(me + d, nsamp)), device_id_type=MESH)

    def unpack(x):
        return jnp.concatenate([x[:, :W], x[:, W:]], axis=0)

    row = lax.broadcasted_iota(jnp.int32, (R, W), 0)
    lane = lax.broadcasted_iota(jnp.int32, (R, W), 1)
    eye = (row == lane).astype(F32)
    hprev[...] = eye
    hown[...] = eye

    @pl.when(has_prev)
    def _():
        total = jnp.zeros((R // 2, 128), F32)
        for d in range(nsamp):
            pltpu.make_async_remote_copy(
                src_ref=sendbuf, dst_ref=got_prev.at[d], send_sem=send_next.at[d],
                recv_sem=recv_prev.at[d], device_id=(mine, me), device_id_type=MESH).wait_recv()
            total = total + got_prev[d]
        hprev[...] = unpack(total)

    @pl.when(has_next)
    def _():
        before = hprev[...]
        wide = jnp.dot(stacked(before), ustack[...], preferred_element_type=F32)
        wh, wl = split(tall_of(wide, pairs))
        both = jnp.dot(uth[...], wh, preferred_element_type=F32)
        both = both + jnp.dot(uth[...], wl, preferred_element_type=F32)
        both = both + jnp.dot(utl[...], wh, preferred_element_type=F32)
        gram = (both[:R, :W] + both[W:W + R, W:]) * (1.0 / N)
        sendbuf[...] = jnp.concatenate([gram[:R // 2], gram[R // 2:]], axis=1)
        for d in range(nsamp):
            next_copy(d).start()
        for d in range(1, nsamp):
            own_copy(d).start()
        total = sendbuf[...]
        for d in range(1, nsamp):
            own_copy(d).wait_recv()
            total = total + got_own[d - 1]
        hown[...] = unpack(total)
        for d in range(nsamp):
            next_copy(d).wait_send()
        for d in range(1, nsamp):
            own_copy(d).wait_send()


def eliminate(mats):
    row = lax.broadcasted_iota(jnp.int32, (R, 128), 0)
    lane = lax.broadcasted_iota(jnp.int32, (R, 128), 1)
    mats = [jnp.concatenate([m, (row == lane).astype(F32)[:, :W]], axis=1) for m in mats]
    for j in range(R):
        nxt = []
        for m in mats:
            pivot = m[j:j + 1, :]
            scaled = pivot * (1.0 / pivot[:, j:j + 1])
            col = jnp.where(row[:, :1] > j, m[:, j:j + 1], 0.0)
            nxt.append(m - col * scaled)
        mats = nxt
    outs = []
    for m in mats:
        diag = jnp.sum(jnp.where(row == lane, m, 0.0), axis=1, keepdims=True)
        outs.append(m * lax.rsqrt(diag))
    return outs


def finish_kernel(pairs, ustack, hprev, hown, out):
    first, second = eliminate([hprev[...], hown[...]])
    carry = first[:, :W]
    inv = second[:, W:]
    wide = jnp.dot(stacked(carry), ustack[...], preferred_element_type=F32)
    tall = tall_of(wide, pairs)
    pad = jnp.zeros((W - R, W), F32)
    inv = jnp.concatenate([inv, pad], axis=0)
    zero = jnp.zeros((W, W), F32)
    diag = jnp.concatenate([jnp.concatenate([inv, zero], axis=1), jnp.concatenate([zero, inv], axis=1)], axis=0)
    out[...] = lax.dot_general(tall, diag, (((1,), (1,)), ((), ())), precision=HIGH, preferred_element_type=F32)


def retract(updated, ncores, nsamp):
    slab = updated.shape[0]
    pairs = slab // 2
    high = lax.reduce_precision(updated, 8, 7)
    low = updated - high
    vm = pl.BlockSpec(memory_space=pltpu.VMEM)

    def wide_of(x):
        x = jnp.pad(x.astype(BF16).reshape(slab, R, R), ((0, 0), (0, W - R), (0, W - R)))
        return x.transpose(1, 0, 2).reshape(W, slab * W)

    def turned(x):
        x = jnp.pad(x.astype(BF16).reshape(pairs, 2, R, R), ((0, 0), (0, 0), (0, 0), (0, W - R)))
        return x.transpose(1, 3, 0, 2).reshape(128, pairs * R)

    wh, wl = wide_of(high), wide_of(low)
    ustack = jnp.concatenate([wh, wl, wh], axis=0)
    square = jax.ShapeDtypeStruct((R, W), F32)
    hprev, hown = pl.pallas_call(
        functools.partial(gram_kernel, ncores, nsamp, pairs),
        out_shape=(square, square),
        in_specs=[vm] * 3,
        out_specs=(vm, vm),
        scratch_shapes=[
            pltpu.VMEM((R // 2, 128), F32),
            pltpu.VMEM((nsamp, R // 2, 128), F32),
            pltpu.VMEM((nsamp - 1, R // 2, 128), F32),
            pltpu.SemaphoreType.DMA((nsamp - 1,)),
            pltpu.SemaphoreType.DMA((nsamp,)),
            pltpu.SemaphoreType.DMA((nsamp - 1,)),
            pltpu.SemaphoreType.DMA((nsamp,)),
        ],
        compiler_params=pltpu.CompilerParams(collective_id=0, has_side_effects=True, vmem_limit_bytes=32 << 20),
        name="gram_chain",
    )(ustack, turned(high), turned(low))
    tall = pl.pallas_call(
        functools.partial(finish_kernel, pairs),
        out_shape=jax.ShapeDtypeStruct((pairs * R, 128), F32),
        in_specs=[vm] * 3,
        out_specs=vm,
        compiler_params=pltpu.CompilerParams(vmem_limit_bytes=32 << 20),
        name="finish",
    )(ustack, hprev, hown)
    tall = tall.reshape(pairs, R, 2, W)[..., :R]
    return tall.transpose(0, 2, 1, 3).reshape(slab, R * R)


def on_device(cores, indices, observed, step_size):
    ncores = lax.axis_size("cores")
    mine = lax.axis_index("cores")
    nsamp = lax.axis_size("samp")
    count = indices.shape[0]
    table = cores[0]
    own_index = lax.dynamic_index_in_dim(indices, mine, 1, keepdims=False)
    mats = jnp.take(table, own_index, axis=0).reshape(count, R, R)
    unit = jnp.broadcast_to((jnp.arange(R) == 0).astype(jnp.float32), (count, R))
    left = unit
    right = unit
    for turn in range(ncores - 1):
        sent = jnp.einsum("sa,sab->sb", left, mats, precision=HIGH)
        moved = from_behind(sent, "cores", 1)
        left = jnp.where(mine == 0, unit, moved)
    for turn in range(ncores - 1):
        sent = jnp.einsum("sab,sb->sa", mats, right, precision=HIGH)
        moved = from_behind(sent, "cores", -1)
        right = jnp.where(mine == ncores - 1, unit, moved)
    predicted = jnp.sum(jnp.einsum("sa,sab->sb", left, mats, precision=HIGH) * right, axis=1)
    residual = predicted - observed
    outer = (left[:, :, None] * (residual[:, None] * right)[:, None, :]).reshape(count, R * R)
    partial_grad = jax.ops.segment_sum(outer, own_index, num_segments=N)
    slab = N // nsamp
    first = lax.axis_index("samp") * slab
    gradient = lax.psum_scatter(partial_grad, "samp", scatter_dimension=0, tiled=True)
    kept = lax.dynamic_slice_in_dim(table, first, slab, 0)
    updated = kept - step_size * gradient
    return retract(updated, ncores, nsamp)[None]


def solution(mesh):
    in_specs = (P("cores", None, None), P("samp", None), P("samp"), P())
    out_specs = P("cores", "samp", None)
    return jax.shard_map(
        on_device, mesh=mesh, in_specs=in_specs, out_specs=out_specs, check_vma=False
    )
```

```python
import functools

import jax
import jax.numpy as jnp
from jax import lax
from jax.experimental import pallas as pl
from jax.experimental.pallas import tpu as pltpu
from jax.sharding import PartitionSpec as P

R = 48
N = 512
W = 64

HIGH = lax.Precision.HIGHEST
MESH = pl.DeviceIdType.MESH
F32 = jnp.float32
BF16 = jnp.bfloat16


def split(x):
    high = x.astype(BF16)
    low = (x - high.astype(F32)).astype(BF16)
    return high, low


def three(x):
    high, low = split(x)
    return jnp.concatenate([high, low, high], axis=0)


def weigh(mat, ustack):
    high, low = split(mat)
    return jnp.dot(jnp.concatenate([high, high, low], axis=1), ustack, preferred_element_type=F32)


def tall_of(wide, pairs):
    return jnp.concatenate([wide[:, 128 * p:128 * p + 128] for p in range(pairs)], axis=0)


def gram_kernel(ncores, nsamp, pairs, uwide, hprev, hown, sendbuf, got_prev, got_own,
                send_own, send_next, recv_own, recv_prev):
    mine = lax.axis_index("cores")
    me = lax.axis_index("samp")
    barrier = pltpu.get_barrier_semaphore()
    has_prev = mine > 0
    has_next = mine < ncores - 1

    def greet(mode, other):
        pl.semaphore_signal(barrier, inc=1, device_id=(mode, other), device_id_type=MESH)

    for d in range(1, nsamp):
        greet(mine, lax.rem(me + d, nsamp))

    @pl.when(has_prev)
    def _():
        for d in range(nsamp):
            greet(mine - 1, lax.rem(me + d, nsamp))

    pl.semaphore_wait(barrier, nsamp - 1 + nsamp * jnp.minimum(ncores - 1 - mine, 1))

    def own_copy(d):
        return pltpu.make_async_remote_copy(
            src_ref=sendbuf, dst_ref=got_own.at[d - 1], send_sem=send_own.at[d - 1],
            recv_sem=recv_own.at[d - 1], device_id=(mine, lax.rem(me + d, nsamp)), device_id_type=MESH)

    def next_copy(d):
        return pltpu.make_async_remote_copy(
            src_ref=sendbuf, dst_ref=got_prev.at[d], send_sem=send_next.at[d],
            recv_sem=recv_prev.at[d], device_id=(mine + 1, lax.rem(me + d, nsamp)), device_id_type=MESH)

    ustack = three(uwide[...])
    uth, utl = split(tall_of(uwide[0:R, :], pairs).T)

    def unpack(x):
        return jnp.concatenate([x[:, :W], x[:, W:]], axis=0)

    row = lax.broadcasted_iota(jnp.int32, (R, W), 0)
    lane = lax.broadcasted_iota(jnp.int32, (R, W), 1)
    eye = (row == lane).astype(F32)
    hprev[...] = eye
    hown[...] = eye

    @pl.when(has_prev)
    def _():
        total = jnp.zeros((R // 2, 128), F32)
        for d in range(nsamp):
            pltpu.make_async_remote_copy(
                src_ref=sendbuf, dst_ref=got_prev.at[d], send_sem=send_next.at[d],
                recv_sem=recv_prev.at[d], device_id=(mine, me), device_id_type=MESH).wait_recv()
            total = total + got_prev[d]
        hprev[...] = unpack(total)

    @pl.when(has_next)
    def _():
        before = hprev[...]
        wh, wl = split(tall_of(weigh(before, ustack), pairs))
        both = jnp.dot(uth, wh, preferred_element_type=F32)
        both = both + jnp.dot(uth, wl, preferred_element_type=F32)
        both = both + jnp.dot(utl, wh, preferred_element_type=F32)
        gram = (both[:R, :W] + both[W:W + R, W:]) * (1.0 / N)
        sendbuf[...] = jnp.concatenate([gram[:R // 2], gram[R // 2:]], axis=1)
        for d in range(nsamp):
            next_copy(d).start()
        for d in range(1, nsamp):
            own_copy(d).start()
        total = sendbuf[...]
        for d in range(1, nsamp):
            own_copy(d).wait_recv()
            total = total + got_own[d - 1]
        hown[...] = unpack(total)
        for d in range(nsamp):
            next_copy(d).wait_send()
        for d in range(1, nsamp):
            own_copy(d).wait_send()


def picker(idx_ref):
    count = idx_ref.shape[1]
    row = lax.broadcasted_iota(jnp.int32, (N, count), 0)
    return jnp.where(row == idx_ref[...], 1.0, 0.0).astype(BF16)


def front_kernel(ncores, table, idx, observed, left_out, right_out, mats, sent_l, sent_r, got_l, got_r, pred,
                 sems):
    mine = lax.axis_index("cores")
    me = lax.axis_index("samp")
    count = idx.shape[1]
    step = 8 * R
    chunk = 256
    first, last = mine == 0, mine == ncores - 1
    barrier = pltpu.get_barrier_semaphore()

    @pl.when(mine > 0)
    def _():
        pl.semaphore_signal(barrier, inc=1, device_id=(mine - 1, me), device_id_type=MESH)

    @pl.when(mine < ncores - 1)
    def _():
        pl.semaphore_signal(barrier, inc=1, device_id=(mine + 1, me), device_id_type=MESH)

    onehot = picker(idx)

    def fill(t, _):
        at = pl.multiple_of(t * step, step)
        part = table[:, pl.ds(at, step)].T
        high, low = split(part)
        mats[pl.ds(at, step), :] = (jnp.dot(high, onehot, preferred_element_type=F32)
                                    + jnp.dot(low, onehot, preferred_element_type=F32))
        return 0

    lax.fori_loop(0, R // 8, fill, 0)
    pl.semaphore_wait(barrier, jnp.minimum(mine, 1) + jnp.minimum(ncores - 1 - mine, 1))
    unit = (lax.broadcasted_iota(jnp.int32, (R, count), 0) == 0).astype(F32)

    copy_l = pltpu.make_async_remote_copy(
        src_ref=sent_l, dst_ref=got_l, send_sem=sems.at[0], recv_sem=sems.at[1],
        device_id=(lax.rem(mine + 1, ncores), me), device_id_type=MESH)
    copy_r = pltpu.make_async_remote_copy(
        src_ref=sent_r, dst_ref=got_r, send_sem=sems.at[2], recv_sem=sems.at[3],
        device_id=(lax.rem(mine + ncores - 1, ncores), me), device_id_type=MESH)

    def go_left():
        @pl.when(first)
        def _():
            got_l[...] = unit
            sent_l[...] = mats[0:R, :]

        @pl.when(mine > 0)
        def _():
            copy_l.wait_recv()

            @pl.when(mine < ncores - 1)
            def _():
                for c in range(0, count, chunk):
                    def add(a, total):
                        return total + got_l[pl.ds(a, 1), c:c + chunk] * mats[pl.ds(pl.multiple_of(a * R, 8), R), c:c + chunk]
                    sent_l[:, c:c + chunk] = lax.fori_loop(0, R, add, jnp.zeros((R, chunk), F32), unroll=4)

        @pl.when(mine < ncores - 1)
        def _():
            copy_l.start()

    def go_right():
        @pl.when(last)
        def _():
            got_r[...] = unit

            def pick(a, _):
                sent_r[pl.ds(a, 1), :] = mats[pl.ds(pl.multiple_of(a * R, 8), 8), :][0:1, :]
                return 0
            lax.fori_loop(0, R, pick, 0)

        @pl.when(mine < ncores - 1)
        def _():
            copy_r.wait_recv()

            @pl.when(mine > 0)
            def _():
                for c in range(0, count, chunk):
                    def one(a, _):
                        m = mats[pl.ds(pl.multiple_of(a * R, 8), R), c:c + chunk] * got_r[:, c:c + chunk]
                        sent_r[pl.ds(a, 1), c:c + chunk] = jnp.sum(m, axis=0, keepdims=True)
                        return 0
                    lax.fori_loop(0, R, one, 0, unroll=4)

        @pl.when(mine > 0)
        def _():
            copy_r.start()

    @pl.when(2 * mine < ncores)
    def _():
        go_left()
        go_right()

    @pl.when(2 * mine >= ncores)
    def _():
        go_right()
        go_left()

    @pl.when(last)
    def _():
        pred[...] = jnp.sum(got_l[...] * sent_r[...], axis=0, keepdims=True)

    @pl.when(mine < ncores - 1)
    def _():
        pred[...] = jnp.sum(sent_l[...] * got_r[...], axis=0, keepdims=True)

    left_out[...] = got_l[...]
    right_out[...] = got_r[...] * (pred[...] - observed[...])

    @pl.when(mine < ncores - 1)
    def _():
        copy_l.wait_send()

    @pl.when(mine > 0)
    def _():
        copy_r.wait_send()


def gradient_kernel(ncores, nsamp, idx, left, right, grad, partial, got, small, got_small, esend, erecv, rsend, rrecv):
    mine = lax.axis_index("cores")
    me = lax.axis_index("samp")
    slab = grad.shape[0]
    half = slab // 2
    step = 8 * R
    wide = R * R // 2
    edge = jnp.logical_or(mine == 0, mine == ncores - 1)
    inner = jnp.logical_not(edge)
    barrier = pltpu.get_barrier_semaphore()
    for d in range(1, nsamp):
        pl.semaphore_signal(barrier, inc=1, device_id=(mine, lax.rem(me + d, nsamp)), device_id_type=MESH)
    onehot = picker(idx)
    nt = (((1,), (1,)), ((), ()))

    def against(vecs):
        high, low = split(vecs)
        return (lax.dot_general(onehot, high, nt, preferred_element_type=F32)
                + lax.dot_general(onehot, low, nt, preferred_element_type=F32))

    odd = lax.rem(me, 2)
    place = (1 - odd) * (me // 2) + odd * (nsamp - 1 - me // 2)

    def at_place(p):
        p = lax.rem(p + 2 * nsamp, nsamp)
        up = jnp.minimum(p // (nsamp // 2), 1)
        return (1 - up) * 2 * p + up * (2 * (nsamp - 1 - p) + 1)

    def ring(direction, c, t, peer):
        return pltpu.make_async_remote_copy(
            src_ref=got.at[direction, c, jnp.maximum(t - 1, 0)], dst_ref=got.at[direction, c, t],
            send_sem=rsend.at[direction, c, t], recv_sem=rrecv.at[direction, c, t],
            device_id=(mine, peer), device_id_type=MESH)

    def rows_of(direction, t):
        owner = at_place(place - 1 - t) if direction == 0 else at_place(place + 1 + t)
        return pl.ds(pl.multiple_of(owner * slab + direction * half, half), half)

    up_peer, down_peer = at_place(place + 1), at_place(place - 1)

    @pl.when(inner)
    def _():
        def block(t, _):
            lhs = left[pl.ds(pl.multiple_of(t * 8, 8), 8), :]
            outer = jnp.concatenate([lhs[a:a + 1, :] * right[...] for a in range(8)], axis=0)
            partial[:, pl.ds(pl.multiple_of(t * step, 128), step)] = against(outer)
            return 0
        lax.fori_loop(0, R // 8, block, 0)

    pl.semaphore_wait(barrier, nsamp - 1)

    @pl.when(inner)
    def _():
        peers = (up_peer, down_peer)
        for c in range(2):
            for direction in range(2):
                pltpu.make_async_remote_copy(
                    src_ref=partial.at[rows_of(direction, 0), pl.ds(c * wide, wide)], dst_ref=got.at[direction, c, 0],
                    send_sem=rsend.at[direction, c, 0], recv_sem=rrecv.at[direction, c, 0],
                    device_id=(mine, peers[direction]), device_id_type=MESH).start()

        def hop(t, _):
            for c in range(2):
                for direction in range(2):
                    ring(direction, c, t - 1, peers[direction]).wait_recv()
                    got[direction, c, t - 1] = (got[direction, c, t - 1]
                                                + partial[rows_of(direction, t), c * wide:c * wide + wide])
                    ring(direction, c, t, peers[direction]).start()
            return 0
        lax.fori_loop(1, nsamp - 1, hop, 0)
        end = nsamp - 2
        for c in range(2):
            for direction in range(2):
                ring(direction, c, end, peers[direction]).wait_recv()
                grad[direction * half:direction * half + half, c * wide:c * wide + wide] = (
                    got[direction, c, end] + partial[rows_of(direction, end + 1), c * wide:c * wide + wide])

        def drain(t, _):
            for c in range(2):
                for direction in range(2):
                    ring(direction, c, t, peers[direction]).wait_send()
            return 0
        lax.fori_loop(0, nsamp - 1, drain, 0)

    @pl.when(edge)
    def _():
        at_first = (mine == 0).astype(F32)
        vec = at_first * right[...] + (1.0 - at_first) * left[...] * right[0:1, :]
        pad = jnp.zeros((128 - R, vec.shape[1]), F32)
        small[...] = against(jnp.concatenate([vec, pad], axis=0))

        def send(d):
            to = lax.rem(me + d, nsamp)
            return pltpu.make_async_remote_copy(
                src_ref=small.at[pl.ds(pl.multiple_of(to * slab, slab), slab)], dst_ref=got_small.at[d - 1],
                send_sem=esend.at[d - 1], recv_sem=erecv.at[d - 1], device_id=(mine, to), device_id_type=MESH)
        for d in range(1, nsamp):
            send(d).start()
        total = small[pl.ds(pl.multiple_of(me * slab, slab), slab), :]
        for d in range(1, nsamp):
            send(d).wait_recv()
            total = total + got_small[d - 1]
        row = lax.broadcasted_iota(jnp.int32, (128, R * R), 0)
        col = lax.broadcasted_iota(jnp.int32, (128, R * R), 1)
        stride = 1 + (R - 1) * jnp.minimum(mine, 1)
        spread = jnp.where(jnp.logical_and(col == row * stride, row < R), 1.0, 0.0).astype(BF16)
        high, low = split(total)
        grad[...] = (jnp.dot(high, spread, preferred_element_type=F32)
                     + jnp.dot(low, spread, preferred_element_type=F32))
        for d in range(1, nsamp):
            send(d).wait_send()


def eliminate(mats):
    row = lax.broadcasted_iota(jnp.int32, (R, 128), 0)
    lane = lax.broadcasted_iota(jnp.int32, (R, 128), 1)
    mats = [jnp.concatenate([m, (row == lane).astype(F32)[:, :W]], axis=1) for m in mats]
    for j in range(R):
        nxt = []
        for m in mats:
            pivot = m[j:j + 1, :]
            scaled = pivot * (1.0 / pivot[:, j:j + 1])
            col = jnp.where(row[:, :1] > j, m[:, j:j + 1], 0.0)
            nxt.append(m - col * scaled)
        mats = nxt
    outs = []
    for m in mats:
        diag = jnp.sum(jnp.where(row == lane, m, 0.0), axis=1, keepdims=True)
        outs.append(m * lax.rsqrt(diag))
    return outs


def finish_kernel(pairs, uwide, hprev, hown, out):
    first, second = eliminate([hprev[...], hown[...]])
    carry = first[:, :W]
    inv = second[:, W:]
    tall = tall_of(weigh(carry, three(uwide[...])), pairs)
    pad = jnp.zeros((W - R, W), F32)
    inv = jnp.concatenate([inv, pad], axis=0)
    zero = jnp.zeros((W, W), F32)
    diag = jnp.concatenate([jnp.concatenate([inv, zero], axis=1), jnp.concatenate([zero, inv], axis=1)], axis=0)
    out[...] = lax.dot_general(tall, diag, (((1,), (1,)), ((), ())), precision=HIGH, preferred_element_type=F32)


def retract(updated, ncores, nsamp):
    slab = updated.shape[0]
    pairs = slab // 2
    vm = pl.BlockSpec(memory_space=pltpu.VMEM)
    uwide = jnp.pad(updated.reshape(slab, R, R).transpose(1, 0, 2), ((0, W - R), (0, 0), (0, W - R)))
    uwide = uwide.reshape(W, slab * W)
    square = jax.ShapeDtypeStruct((R, W), F32)
    hprev, hown = pl.pallas_call(
        functools.partial(gram_kernel, ncores, nsamp, pairs),
        out_shape=(square, square),
        in_specs=[vm],
        out_specs=(vm, vm),
        scratch_shapes=[
            pltpu.VMEM((R // 2, 128), F32),
            pltpu.VMEM((nsamp, R // 2, 128), F32),
            pltpu.VMEM((nsamp - 1, R // 2, 128), F32),
            pltpu.SemaphoreType.DMA((nsamp - 1,)),
            pltpu.SemaphoreType.DMA((nsamp,)),
            pltpu.SemaphoreType.DMA((nsamp - 1,)),
            pltpu.SemaphoreType.DMA((nsamp,)),
        ],
        compiler_params=pltpu.CompilerParams(collective_id=0, has_side_effects=True, vmem_limit_bytes=32 << 20),
        name="gram_chain",
    )(uwide)
    tall = pl.pallas_call(
        functools.partial(finish_kernel, pairs),
        out_shape=jax.ShapeDtypeStruct((pairs * R, 128), F32),
        in_specs=[vm] * 3,
        out_specs=vm,
        compiler_params=pltpu.CompilerParams(vmem_limit_bytes=32 << 20),
        name="finish",
    )(uwide, hprev, hown)
    tall = tall.reshape(pairs, R, 2, W)[..., :R]
    return tall.transpose(0, 2, 1, 3).reshape(slab, R * R)


def on_device(cores, indices, observed, step_size):
    ncores = lax.axis_size("cores")
    mine = lax.axis_index("cores")
    nsamp = lax.axis_size("samp")
    count = indices.shape[0]
    table = cores[0]
    own_index = lax.dynamic_index_in_dim(indices, mine, 1, keepdims=False)
    slab = N // nsamp
    first = lax.axis_index("samp") * slab
    vm = pl.BlockSpec(memory_space=pltpu.VMEM)
    vectors = jax.ShapeDtypeStruct((R, count), F32)
    left, right = pl.pallas_call(
        functools.partial(front_kernel, ncores),
        out_shape=(vectors, vectors),
        in_specs=[vm] * 3,
        out_specs=(vm, vm),
        scratch_shapes=[
            pltpu.VMEM((R * R, count), F32),
            pltpu.VMEM((R, count), F32),
            pltpu.VMEM((R, count), F32),
            pltpu.VMEM((R, count), F32),
            pltpu.VMEM((R, count), F32),
            pltpu.VMEM((1, count), F32),
            pltpu.SemaphoreType.DMA((4,)),
        ],
        compiler_params=pltpu.CompilerParams(collective_id=1, has_side_effects=True, vmem_limit_bytes=48 << 20),
        name="sample_vectors",
    )(table, own_index.reshape(1, count), observed.reshape(1, count))
    gradient = pl.pallas_call(
        functools.partial(gradient_kernel, ncores, nsamp),
        out_shape=jax.ShapeDtypeStruct((slab, R * R), F32),
        in_specs=[vm] * 3,
        out_specs=vm,
        scratch_shapes=[
            pltpu.VMEM((N, R * R), F32),
            pltpu.VMEM((2, 2, nsamp - 1, slab // 2, R * R // 2), F32),
            pltpu.VMEM((N, 128), F32),
            pltpu.VMEM((nsamp - 1, slab, 128), F32),
            pltpu.SemaphoreType.DMA((nsamp - 1,)),
            pltpu.SemaphoreType.DMA((nsamp - 1,)),
            pltpu.SemaphoreType.DMA((2, 2, nsamp - 1)),
            pltpu.SemaphoreType.DMA((2, 2, nsamp - 1)),
        ],
        compiler_params=pltpu.CompilerParams(collective_id=2, has_side_effects=True, vmem_limit_bytes=48 << 20),
        name="gradient_sum",
    )(own_index.reshape(1, count), left, right)
    kept = lax.dynamic_slice_in_dim(table, first, slab, 0)
    updated = kept - step_size * gradient
    return retract(updated, ncores, nsamp)[None]


def solution(mesh):
    in_specs = (P("cores", None, None), P("samp", None), P("samp"), P())
    out_specs = P("cores", "samp", None)
    return jax.shard_map(
        on_device, mesh=mesh, in_specs=in_specs, out_specs=out_specs, check_vma=False
    )
```

```python
import functools

import jax
import jax.numpy as jnp
from jax import lax
from jax.experimental import pallas as pl
from jax.experimental.pallas import tpu as pltpu
from jax.sharding import PartitionSpec as P

R = 48
N = 512
W = 64

HIGH = lax.Precision.HIGHEST
MESH = pl.DeviceIdType.MESH
F32 = jnp.float32
BF16 = jnp.bfloat16


def split(x):
    high = x.astype(BF16)
    low = (x - high.astype(F32)).astype(BF16)
    return high, low


def three(x):
    high, low = split(x)
    return jnp.concatenate([high, low, high], axis=0)


def weigh(mat, ustack):
    high, low = split(mat)
    return jnp.dot(jnp.concatenate([high, high, low], axis=1), ustack, preferred_element_type=F32)


def tall_of(wide, pairs):
    return jnp.concatenate([wide[:, 128 * p:128 * p + 128] for p in range(pairs)], axis=0)


def gram_kernel(ncores, nsamp, pairs, uwide, hprev, hown, sendbuf, got_prev, got_own,
                send_own, send_next, recv_own, recv_prev):
    mine = lax.axis_index("cores")
    me = lax.axis_index("samp")
    barrier = pltpu.get_barrier_semaphore()
    has_prev = mine > 0
    has_next = mine < ncores - 1

    def greet(mode, other):
        pl.semaphore_signal(barrier, inc=1, device_id=(mode, other), device_id_type=MESH)

    for d in range(1, nsamp):
        greet(mine, lax.rem(me + d, nsamp))

    @pl.when(has_prev)
    def _():
        for d in range(nsamp):
            greet(mine - 1, lax.rem(me + d, nsamp))

    def own_copy(d):
        return pltpu.make_async_remote_copy(
            src_ref=sendbuf, dst_ref=got_own.at[d - 1], send_sem=send_own.at[d - 1],
            recv_sem=recv_own.at[d - 1], device_id=(mine, lax.rem(me + d, nsamp)), device_id_type=MESH)

    def next_copy(d):
        return pltpu.make_async_remote_copy(
            src_ref=sendbuf, dst_ref=got_prev.at[d], send_sem=send_next.at[d],
            recv_sem=recv_prev.at[d], device_id=(mine + 1, lax.rem(me + d, nsamp)), device_id_type=MESH)

    ustack = three(uwide[...])
    uth, utl = split(tall_of(uwide[0:R, :], pairs).T)

    def unpack(x):
        return jnp.concatenate([x[:, :W], x[:, W:]], axis=0)

    row = lax.broadcasted_iota(jnp.int32, (R, W), 0)
    lane = lax.broadcasted_iota(jnp.int32, (R, W), 1)
    eye = (row == lane).astype(F32)
    hprev[...] = eye
    hown[...] = eye

    @pl.when(has_prev)
    def _():
        total = jnp.zeros((R // 2, 128), F32)
        for d in range(nsamp):
            pltpu.make_async_remote_copy(
                src_ref=sendbuf, dst_ref=got_prev.at[d], send_sem=send_next.at[d],
                recv_sem=recv_prev.at[d], device_id=(mine, me), device_id_type=MESH).wait_recv()
            total = total + got_prev[d]
        hprev[...] = unpack(total)

    @pl.when(jnp.logical_not(has_next))
    def _():
        pl.semaphore_wait(barrier, nsamp - 1)

    @pl.when(has_next)
    def _():
        before = hprev[...]
        wh, wl = split(tall_of(weigh(before, ustack), pairs))
        both = jnp.dot(uth, wh, preferred_element_type=F32)
        both = both + jnp.dot(uth, wl, preferred_element_type=F32)
        both = both + jnp.dot(utl, wh, preferred_element_type=F32)
        gram = (both[:R, :W] + both[W:W + R, W:]) * (1.0 / N)
        sendbuf[...] = jnp.concatenate([gram[:R // 2], gram[R // 2:]], axis=1)
        pl.semaphore_wait(barrier, 2 * nsamp - 1)
        for d in range(nsamp):
            next_copy(d).start()
        for d in range(1, nsamp):
            own_copy(d).start()
        total = sendbuf[...]
        for d in range(1, nsamp):
            own_copy(d).wait_recv()
            total = total + got_own[d - 1]
        hown[...] = unpack(total)
        for d in range(nsamp):
            next_copy(d).wait_send()
        for d in range(1, nsamp):
            own_copy(d).wait_send()


def picker(idx_ref):
    count = idx_ref.shape[1]
    row = lax.broadcasted_iota(jnp.int32, (N, count), 0)
    return jnp.where(row == idx_ref[...], 1.0, 0.0).astype(BF16)


def front_kernel(ncores, cores, idx, observed, left_out, right_out, table, mats, sent_l, sent_r, got_l, got_r, pred,
                 loads, sems):
    mine = lax.axis_index("cores")
    me = lax.axis_index("samp")
    count = idx.shape[1]
    step = 8 * R
    blocks = R // 8
    chunk = 256
    chunks = count // chunk
    first, last = mine == 0, mine == ncores - 1
    inner = jnp.logical_not(jnp.logical_or(first, last))
    barrier = pltpu.get_barrier_semaphore()

    def load(t):
        lanes = pl.ds(pl.multiple_of(t * step, 128), step)
        return pltpu.make_async_copy(cores.at[0, :, lanes], table.at[:, lanes], loads.at[t])

    for t in range(blocks):
        load(t).start()

    @pl.when(mine > 0)
    def _():
        pl.semaphore_signal(barrier, inc=1, device_id=(mine - 1, me), device_id_type=MESH)

    @pl.when(mine < ncores - 1)
    def _():
        pl.semaphore_signal(barrier, inc=1, device_id=(mine + 1, me), device_id_type=MESH)

    onehot = picker(idx)
    unit = (lax.broadcasted_iota(jnp.int32, (R, count), 0) == 0).astype(F32)

    def picked(part):
        high, low = split(part.T)
        return (jnp.dot(high, onehot, preferred_element_type=F32)
                + jnp.dot(low, onehot, preferred_element_type=F32))

    @pl.when(first)
    def _():
        load(0).wait()
        sent_l[...] = picked(table[:, 0:128])[0:R]
        got_l[...] = unit
        for t in range(1, blocks):
            load(t).wait()

    @pl.when(last)
    def _():
        for t in range(blocks):
            load(t).wait()
        row = lax.broadcasted_iota(jnp.int32, (R * R, 128), 0)
        col = lax.broadcasted_iota(jnp.int32, (R * R, 128), 1)
        heads = jnp.where(jnp.logical_and(row == col * R, col < R), 1.0, 0.0).astype(BF16)
        high, low = split(table[...])
        part = jnp.dot(high, heads, preferred_element_type=F32) + jnp.dot(low, heads, preferred_element_type=F32)
        sent_r[...] = picked(part)[0:R]
        got_r[...] = unit

    @pl.when(inner)
    def _():
        def fill(t, _):
            load(t).wait()
            at = pl.multiple_of(t * step, step)
            mats[pl.ds(at, step), :] = picked(table[:, pl.ds(at, step)])
            return 0
        lax.fori_loop(0, blocks, fill, 0)

    pl.semaphore_wait(barrier, jnp.minimum(mine, 1) + jnp.minimum(ncores - 1 - mine, 1))

    def copy_l(n):
        lanes = pl.ds(n * chunk, chunk)
        return pltpu.make_async_remote_copy(
            src_ref=sent_l.at[:, lanes], dst_ref=got_l.at[:, lanes], send_sem=sems.at[0, n], recv_sem=sems.at[1, n],
            device_id=(lax.rem(mine + 1, ncores), me), device_id_type=MESH)

    def copy_r(n):
        lanes = pl.ds(n * chunk, chunk)
        return pltpu.make_async_remote_copy(
            src_ref=sent_r.at[:, lanes], dst_ref=got_r.at[:, lanes], send_sem=sems.at[2, n], recv_sem=sems.at[3, n],
            device_id=(lax.rem(mine + ncores - 1, ncores), me), device_id_type=MESH)

    def pass_left():
        for n in range(chunks):
            c = n * chunk
            copy_l(n).wait_recv()

            def add(a, total):
                return total + got_l[pl.ds(a, 1), c:c + chunk] * mats[pl.ds(pl.multiple_of(a * R, 8), R), c:c + chunk]
            sent_l[:, c:c + chunk] = lax.fori_loop(0, R, add, jnp.zeros((R, chunk), F32), unroll=4)
            copy_l(n).start()

    def pass_right():
        for n in range(chunks):
            c = n * chunk
            copy_r(n).wait_recv()

            def one(a, _):
                m = mats[pl.ds(pl.multiple_of(a * R, 8), R), c:c + chunk] * got_r[:, c:c + chunk]
                sent_r[pl.ds(a, 1), c:c + chunk] = jnp.sum(m, axis=0, keepdims=True)
                return 0
            lax.fori_loop(0, R, one, 0, unroll=4)
            copy_r(n).start()

    @pl.when(first)
    def _():
        for n in range(chunks):
            copy_l(n).start()
        for n in range(chunks):
            copy_r(n).wait_recv()

    @pl.when(last)
    def _():
        for n in range(chunks):
            copy_r(n).start()
        for n in range(chunks):
            copy_l(n).wait_recv()

    @pl.when(jnp.logical_and(inner, 2 * mine < ncores))
    def _():
        pass_left()
        pass_right()

    @pl.when(jnp.logical_and(inner, 2 * mine >= ncores))
    def _():
        pass_right()
        pass_left()

    @pl.when(last)
    def _():
        pred[...] = jnp.sum(got_l[...] * sent_r[...], axis=0, keepdims=True)

    @pl.when(mine < ncores - 1)
    def _():
        pred[...] = jnp.sum(sent_l[...] * got_r[...], axis=0, keepdims=True)

    left_out[...] = got_l[...]
    right_out[...] = got_r[...] * (pred[...] - observed[...])

    @pl.when(mine < ncores - 1)
    def _():
        for n in range(chunks):
            copy_l(n).wait_send()

    @pl.when(mine > 0)
    def _():
        for n in range(chunks):
            copy_r(n).wait_send()


def gradient_kernel(ncores, nsamp, idx, left, right, cores, rate, updated, partial, got, small, got_small, kept,
                    ksem, esend, erecv, rsend, rrecv):
    mine = lax.axis_index("cores")
    me = lax.axis_index("samp")
    slab = updated.shape[0]
    half = slab // 2
    step = 8 * R
    parts = got.shape[1]
    wide = R * R // parts
    edge = jnp.logical_or(mine == 0, mine == ncores - 1)
    inner = jnp.logical_not(edge)
    barrier = pltpu.get_barrier_semaphore()
    for d in range(1, nsamp):
        pl.semaphore_signal(barrier, inc=1, device_id=(mine, lax.rem(me + d, nsamp)), device_id_type=MESH)
    keep = pltpu.make_async_copy(cores.at[0, pl.ds(pl.multiple_of(me * slab, slab), slab)], kept, ksem)
    keep.start()
    onehot = picker(idx)
    nt = (((1,), (1,)), ((), ()))

    def against(vecs):
        high, low = split(vecs)
        return (lax.dot_general(onehot, high, nt, preferred_element_type=F32)
                + lax.dot_general(onehot, low, nt, preferred_element_type=F32))

    odd = lax.rem(me, 2)
    place = (1 - odd) * (me // 2) + odd * (nsamp - 1 - me // 2)

    def at_place(p):
        p = lax.rem(p + 2 * nsamp, nsamp)
        up = jnp.minimum(p // (nsamp // 2), 1)
        return (1 - up) * 2 * p + up * (2 * (nsamp - 1 - p) + 1)

    def ring(direction, c, t, peer):
        return pltpu.make_async_remote_copy(
            src_ref=got.at[direction, c, jnp.maximum(t - 1, 0)], dst_ref=got.at[direction, c, t],
            send_sem=rsend.at[direction, c, t], recv_sem=rrecv.at[direction, c, t],
            device_id=(mine, peer), device_id_type=MESH)

    def rows_of(direction, t):
        owner = at_place(place - 1 - t) if direction == 0 else at_place(place + 1 + t)
        return pl.ds(pl.multiple_of(owner * slab + direction * half, half), half)

    up_peer, down_peer = at_place(place + 1), at_place(place - 1)

    def block(t, _):
        lhs = left[pl.ds(pl.multiple_of(t * 8, 8), 8), :]
        outer = jnp.concatenate([lhs[a:a + 1, :] * right[...] for a in range(8)], axis=0)
        partial[:, pl.ds(pl.multiple_of(t * step, 128), step)] = against(outer)
        return 0

    each = R // 8 // parts

    @pl.when(inner)
    def _():
        lax.fori_loop(0, each, block, 0)

    keep.wait()
    pl.semaphore_wait(barrier, nsamp - 1)

    @pl.when(inner)
    def _():
        peers = (up_peer, down_peer)

        def begin(c):
            for direction in range(2):
                pltpu.make_async_remote_copy(
                    src_ref=partial.at[rows_of(direction, 0), pl.ds(c * wide, wide)], dst_ref=got.at[direction, c, 0],
                    send_sem=rsend.at[direction, c, 0], recv_sem=rrecv.at[direction, c, 0],
                    device_id=(mine, peers[direction]), device_id_type=MESH).start()

        def hop(c, t):
            for direction in range(2):
                ring(direction, c, t - 1, peers[direction]).wait_recv()
                got[direction, c, t - 1] = (got[direction, c, t - 1]
                                            + partial[rows_of(direction, t), c * wide:c * wide + wide])
                ring(direction, c, t, peers[direction]).start()

        def finish(c):
            end = nsamp - 2
            for direction in range(2):
                ring(direction, c, end, peers[direction]).wait_recv()
                here = (slice(direction * half, direction * half + half), slice(c * wide, c * wide + wide))
                updated[here] = kept[here] - rate[0, 0] * (
                    got[direction, c, end] + partial[rows_of(direction, end + 1), c * wide:c * wide + wide])

        for turn in range(parts):
            if turn > 0:
                lax.fori_loop(turn * each, (turn + 1) * each, block, 0)
            begin(turn)
            for c in range(turn):
                if turn - c <= nsamp - 2:
                    hop(c, turn - c)

        def steady(turn, _):
            for c in range(parts):
                hop(c, turn - c)
            return 0
        lax.fori_loop(parts, nsamp - 1, steady, 0)
        for turn in range(max(parts, nsamp - 1), parts + nsamp - 1):
            for c in range(parts):
                if turn - c <= nsamp - 2:
                    hop(c, turn - c)
                elif turn - c == nsamp - 1:
                    finish(c)

        def drain(t, _):
            for c in range(parts):
                for direction in range(2):
                    ring(direction, c, t, peers[direction]).wait_send()
            return 0
        lax.fori_loop(0, nsamp - 1, drain, 0)

    @pl.when(edge)
    def _():
        at_first = (mine == 0).astype(F32)
        vec = at_first * right[...] + (1.0 - at_first) * left[...] * right[0:1, :]
        pad = jnp.zeros((128 - R, vec.shape[1]), F32)
        small[...] = against(jnp.concatenate([vec, pad], axis=0))

        def send(d):
            to = lax.rem(me + d, nsamp)
            return pltpu.make_async_remote_copy(
                src_ref=small.at[pl.ds(pl.multiple_of(to * slab, slab), slab)], dst_ref=got_small.at[d - 1],
                send_sem=esend.at[d - 1], recv_sem=erecv.at[d - 1], device_id=(mine, to), device_id_type=MESH)
        for d in range(1, nsamp):
            send(d).start()
        total = small[pl.ds(pl.multiple_of(me * slab, slab), slab), :]
        for d in range(1, nsamp):
            send(d).wait_recv()
            total = total + got_small[d - 1]
        row = lax.broadcasted_iota(jnp.int32, (128, R * R), 0)
        col = lax.broadcasted_iota(jnp.int32, (128, R * R), 1)
        stride = 1 + (R - 1) * jnp.minimum(mine, 1)
        spread = jnp.where(jnp.logical_and(col == row * stride, row < R), 1.0, 0.0).astype(BF16)
        high, low = split(total)
        updated[...] = kept[...] - rate[0, 0] * (jnp.dot(high, spread, preferred_element_type=F32)
                                                 + jnp.dot(low, spread, preferred_element_type=F32))
        for d in range(1, nsamp):
            send(d).wait_send()


def eliminate(mats):
    row = lax.broadcasted_iota(jnp.int32, (R, 128), 0)
    lane = lax.broadcasted_iota(jnp.int32, (R, 128), 1)
    mats = [jnp.concatenate([m, (row == lane).astype(F32)[:, :W]], axis=1) for m in mats]
    for j in range(0, R, 2):
        nxt = []
        for m in mats:
            col0 = jnp.broadcast_to(m[:, j:j + 1], (R, 128))
            col1 = jnp.broadcast_to(m[:, j + 1:j + 2], (R, 128))
            inv0 = 1.0 / col0[j:j + 1]
            ratio = col0[j + 1:j + 2] * inv0
            inv1 = 1.0 / (col1[j + 1:j + 2] - ratio * col0[j + 1:j + 2])
            row0 = m[j:j + 1]
            row1 = m[j + 1:j + 2] - ratio * row0
            col1 = jnp.where(row > j + 1, col1 - col0 * ratio, 0.0)
            col0 = jnp.where(row > j, col0, 0.0)
            nxt.append(m - col0 * (row0 * inv0) - col1 * (row1 * inv1))
        mats = nxt
    outs = []
    for m in mats:
        diag = jnp.sum(jnp.where(row == lane, m, 0.0), axis=1, keepdims=True)
        outs.append(m * lax.rsqrt(diag))
    return outs


def finish_kernel(pairs, uwide, hprev, hown, out):
    first, second = eliminate([hprev[...], hown[...]])
    carry = first[:, :W]
    inv = second[:, W:]
    tall = tall_of(weigh(carry, three(uwide[...])), pairs)
    pad = jnp.zeros((W - R, W), F32)
    inv = jnp.concatenate([inv, pad], axis=0)
    zero = jnp.zeros((W, W), F32)
    diag = jnp.concatenate([jnp.concatenate([inv, zero], axis=1), jnp.concatenate([zero, inv], axis=1)], axis=0)
    out[...] = lax.dot_general(tall, diag, (((1,), (1,)), ((), ())), precision=HIGH, preferred_element_type=F32)


def retract(updated, ncores, nsamp):
    slab = updated.shape[0]
    pairs = slab // 2
    vm = pl.BlockSpec(memory_space=pltpu.VMEM)
    uwide = jnp.pad(updated.reshape(slab, R, R).transpose(1, 0, 2), ((0, W - R), (0, 0), (0, W - R)))
    uwide = uwide.reshape(W, slab * W)
    square = jax.ShapeDtypeStruct((R, W), F32)
    hprev, hown = pl.pallas_call(
        functools.partial(gram_kernel, ncores, nsamp, pairs),
        out_shape=(square, square),
        in_specs=[vm],
        out_specs=(vm, vm),
        scratch_shapes=[
            pltpu.VMEM((R // 2, 128), F32),
            pltpu.VMEM((nsamp, R // 2, 128), F32),
            pltpu.VMEM((nsamp - 1, R // 2, 128), F32),
            pltpu.SemaphoreType.DMA((nsamp - 1,)),
            pltpu.SemaphoreType.DMA((nsamp,)),
            pltpu.SemaphoreType.DMA((nsamp - 1,)),
            pltpu.SemaphoreType.DMA((nsamp,)),
        ],
        compiler_params=pltpu.CompilerParams(collective_id=0, has_side_effects=True, vmem_limit_bytes=32 << 20),
        name="gram_chain",
    )(uwide)
    tall = pl.pallas_call(
        functools.partial(finish_kernel, pairs),
        out_shape=jax.ShapeDtypeStruct((pairs * R, 128), F32),
        in_specs=[vm] * 3,
        out_specs=vm,
        compiler_params=pltpu.CompilerParams(vmem_limit_bytes=32 << 20),
        name="finish",
    )(uwide, hprev, hown)
    tall = tall.reshape(pairs, R, 2, W)[..., :R]
    return tall.transpose(0, 2, 1, 3).reshape(slab, R * R)


def on_device(cores, indices, observed, step_size):
    ncores = lax.axis_size("cores")
    mine = lax.axis_index("cores")
    nsamp = lax.axis_size("samp")
    count = indices.shape[0]
    own_index = lax.dynamic_index_in_dim(indices, mine, 1, keepdims=False)
    slab = N // nsamp
    parts = 3
    vm = pl.BlockSpec(memory_space=pltpu.VMEM)
    vectors = jax.ShapeDtypeStruct((R, count), F32)
    left, right = pl.pallas_call(
        functools.partial(front_kernel, ncores),
        out_shape=(vectors, vectors),
        in_specs=[pl.BlockSpec(memory_space=pl.ANY), vm, vm],
        out_specs=(vm, vm),
        scratch_shapes=[
            pltpu.VMEM((N, R * R), F32),
            pltpu.VMEM((R * R, count), F32),
            pltpu.VMEM((R, count), F32),
            pltpu.VMEM((R, count), F32),
            pltpu.VMEM((R, count), F32),
            pltpu.VMEM((R, count), F32),
            pltpu.VMEM((1, count), F32),
            pltpu.SemaphoreType.DMA((R // 8,)),
            pltpu.SemaphoreType.DMA((4, count // 256)),
        ],
        compiler_params=pltpu.CompilerParams(collective_id=1, has_side_effects=True, vmem_limit_bytes=48 << 20),
        name="sample_vectors",
    )(cores, own_index.reshape(1, count), observed.reshape(1, count))
    updated = pl.pallas_call(
        functools.partial(gradient_kernel, ncores, nsamp),
        out_shape=jax.ShapeDtypeStruct((slab, R * R), F32),
        in_specs=[vm] * 3 + [pl.BlockSpec(memory_space=pl.ANY), pl.BlockSpec(memory_space=pltpu.SMEM)],
        out_specs=vm,
        scratch_shapes=[
            pltpu.VMEM((N, R * R), F32),
            pltpu.VMEM((2, parts, nsamp - 1, slab // 2, R * R // parts), F32),
            pltpu.VMEM((N, 128), F32),
            pltpu.VMEM((nsamp - 1, slab, 128), F32),
            pltpu.VMEM((slab, R * R), F32),
            pltpu.SemaphoreType.DMA,
            pltpu.SemaphoreType.DMA((nsamp - 1,)),
            pltpu.SemaphoreType.DMA((nsamp - 1,)),
            pltpu.SemaphoreType.DMA((2, parts, nsamp - 1)),
            pltpu.SemaphoreType.DMA((2, parts, nsamp - 1)),
        ],
        compiler_params=pltpu.CompilerParams(collective_id=2, has_side_effects=True, vmem_limit_bytes=48 << 20),
        name="gradient_sum",
    )(own_index.reshape(1, count), left, right, cores, step_size.reshape(1, 1))
    return retract(updated, ncores, nsamp)[None]


def solution(mesh):
    in_specs = (P("cores", None, None), P("samp", None), P("samp"), P())
    out_specs = P("cores", "samp", None)
    return jax.shard_map(
        on_device, mesh=mesh, in_specs=in_specs, out_specs=out_specs, check_vma=False
    )
```

```python
import functools

import jax
import jax.numpy as jnp
from jax import lax
from jax.experimental import pallas as pl
from jax.experimental.pallas import tpu as pltpu
from jax.sharding import PartitionSpec as P

R = 48
N = 512
W = 64

HIGH = lax.Precision.HIGHEST
MESH = pl.DeviceIdType.MESH
F32 = jnp.float32
BF16 = jnp.bfloat16


def split(x):
    high = x.astype(BF16)
    low = (x - high.astype(F32)).astype(BF16)
    return high, low


def three(x):
    high, low = split(x)
    return jnp.concatenate([high, low, high], axis=0)


def weigh(mat, ustack):
    high, low = split(mat)
    return jnp.dot(jnp.concatenate([high, high, low], axis=1), ustack, preferred_element_type=F32)


def tall_of(wide, pairs):
    return jnp.concatenate([wide[:, 128 * p:128 * p + 128] for p in range(pairs)], axis=0)


def gram_kernel(ncores, nsamp, pairs, uwide, hprev, hown, sendbuf, got_prev, got_own,
                send_own, send_next, recv_own, recv_prev):
    mine = lax.axis_index("cores")
    me = lax.axis_index("samp")
    barrier = pltpu.get_barrier_semaphore()
    has_prev = mine > 0
    has_next = mine < ncores - 1

    def greet(mode, other):
        pl.semaphore_signal(barrier, inc=1, device_id=(mode, other), device_id_type=MESH)

    for d in range(1, nsamp):
        greet(mine, lax.rem(me + d, nsamp))

    @pl.when(has_prev)
    def _():
        for d in range(nsamp):
            greet(mine - 1, lax.rem(me + d, nsamp))

    def own_copy(d):
        return pltpu.make_async_remote_copy(
            src_ref=sendbuf, dst_ref=got_own.at[d - 1], send_sem=send_own.at[d - 1],
            recv_sem=recv_own.at[d - 1], device_id=(mine, lax.rem(me + d, nsamp)), device_id_type=MESH)

    def next_copy(d):
        return pltpu.make_async_remote_copy(
            src_ref=sendbuf, dst_ref=got_prev.at[d], send_sem=send_next.at[d],
            recv_sem=recv_prev.at[d], device_id=(mine + 1, lax.rem(me + d, nsamp)), device_id_type=MESH)

    ustack = three(uwide[...])
    uth, utl = split(tall_of(uwide[0:R, :], pairs).T)

    def unpack(x):
        return jnp.concatenate([x[:, :W], x[:, W:]], axis=0)

    row = lax.broadcasted_iota(jnp.int32, (R, W), 0)
    lane = lax.broadcasted_iota(jnp.int32, (R, W), 1)
    eye = (row == lane).astype(F32)
    hprev[...] = eye
    hown[...] = eye

    @pl.when(has_prev)
    def _():
        total = jnp.zeros((R // 2, 128), F32)
        for d in range(nsamp):
            pltpu.make_async_remote_copy(
                src_ref=sendbuf, dst_ref=got_prev.at[d], send_sem=send_next.at[d],
                recv_sem=recv_prev.at[d], device_id=(mine, me), device_id_type=MESH).wait_recv()
            total = total + got_prev[d]
        hprev[...] = unpack(total)

    @pl.when(jnp.logical_not(has_next))
    def _():
        pl.semaphore_wait(barrier, nsamp - 1)

    @pl.when(has_next)
    def _():
        before = hprev[...]
        wh, wl = split(tall_of(weigh(before, ustack), pairs))
        both = jnp.dot(uth, wh, preferred_element_type=F32)
        both = both + jnp.dot(uth, wl, preferred_element_type=F32)
        both = both + jnp.dot(utl, wh, preferred_element_type=F32)
        gram = (both[:R, :W] + both[W:W + R, W:]) * (1.0 / N)
        sendbuf[...] = jnp.concatenate([gram[:R // 2], gram[R // 2:]], axis=1)
        pl.semaphore_wait(barrier, 2 * nsamp - 1)
        for d in range(nsamp):
            next_copy(d).start()
        for d in range(1, nsamp):
            own_copy(d).start()
        total = sendbuf[...]
        for d in range(1, nsamp):
            own_copy(d).wait_recv()
            total = total + got_own[d - 1]
        hown[...] = unpack(total)
        for d in range(nsamp):
            next_copy(d).wait_send()
        for d in range(1, nsamp):
            own_copy(d).wait_send()


def picker(idx_ref):
    count = idx_ref.shape[1]
    row = lax.broadcasted_iota(jnp.int32, (N, count), 0)
    return jnp.where(row == idx_ref[...], 1.0, 0.0).astype(BF16)


def front_kernel(ncores, nsamp, room, cores, idx, every, observed, left_out, right_out, over, table, mats, sent_l, sent_r, got_l, got_r, pred,
                 flag, got_flag, loads, sems, fsend, frecv):
    mine = lax.axis_index("cores")
    me = lax.axis_index("samp")
    count = idx.shape[1]
    step = 8 * R
    blocks = R // 8
    chunk = 256
    chunks = count // chunk
    first, last = mine == 0, mine == ncores - 1
    inner = jnp.logical_not(jnp.logical_or(first, last))
    barrier = pltpu.get_barrier_semaphore()

    def load(t):
        lanes = pl.ds(pl.multiple_of(t * step, 128), step)
        return pltpu.make_async_copy(cores.at[0, :, lanes], table.at[:, lanes], loads.at[t])

    for t in range(blocks):
        load(t).start()

    @pl.when(mine > 0)
    def _():
        pl.semaphore_signal(barrier, inc=1, device_id=(mine - 1, me), device_id_type=MESH)

    @pl.when(mine < ncores - 1)
    def _():
        pl.semaphore_signal(barrier, inc=1, device_id=(mine + 1, me), device_id_type=MESH)

    for d in range(1, nsamp):
        pl.semaphore_signal(barrier, inc=1, device_id=(mine, lax.rem(me + d, nsamp)), device_id_type=MESH)

    def tell(d):
        return pltpu.make_async_remote_copy(
            src_ref=flag, dst_ref=got_flag.at[d - 1], send_sem=fsend.at[d - 1], recv_sem=frecv.at[d - 1],
            device_id=(mine, lax.rem(me + d, nsamp)), device_id_type=MESH)

    most = jnp.zeros((nsamp, 1), F32)
    owner = lax.broadcasted_iota(jnp.int32, (nsamp, count), 0)
    for m in range(ncores):
        member = jnp.where(every[m:m + 1, :] // (N // nsamp) == owner, 1.0, 0.0)
        most = jnp.maximum(most, jnp.sum(member, axis=1, keepdims=True))
    most = jnp.max(most, axis=0, keepdims=True)
    flag[...] = jnp.broadcast_to(jnp.where(most > room, 1.0, 0.0), (8, 128))

    onehot = picker(idx)
    unit = (lax.broadcasted_iota(jnp.int32, (R, count), 0) == 0).astype(F32)

    def picked(part):
        high, low = split(part.T)
        return (jnp.dot(high, onehot, preferred_element_type=F32)
                + jnp.dot(low, onehot, preferred_element_type=F32))

    @pl.when(first)
    def _():
        load(0).wait()
        sent_l[...] = picked(table[:, 0:128])[0:R]
        got_l[...] = unit
        for t in range(1, blocks):
            load(t).wait()

    @pl.when(last)
    def _():
        for t in range(blocks):
            load(t).wait()
        row = lax.broadcasted_iota(jnp.int32, (R * R, 128), 0)
        col = lax.broadcasted_iota(jnp.int32, (R * R, 128), 1)
        heads = jnp.where(jnp.logical_and(row == col * R, col < R), 1.0, 0.0).astype(BF16)
        high, low = split(table[...])
        part = jnp.dot(high, heads, preferred_element_type=F32) + jnp.dot(low, heads, preferred_element_type=F32)
        sent_r[...] = picked(part)[0:R]
        got_r[...] = unit

    @pl.when(inner)
    def _():
        def fill(t, _):
            load(t).wait()
            at = pl.multiple_of(t * step, step)
            mats[pl.ds(at, step), :] = picked(table[:, pl.ds(at, step)])
            return 0
        lax.fori_loop(0, blocks, fill, 0)

    pl.semaphore_wait(barrier, nsamp - 1 + jnp.minimum(mine, 1) + jnp.minimum(ncores - 1 - mine, 1))
    for d in range(1, nsamp):
        tell(d).start()

    def copy_l(n):
        lanes = pl.ds(n * chunk, chunk)
        return pltpu.make_async_remote_copy(
            src_ref=sent_l.at[:, lanes], dst_ref=got_l.at[:, lanes], send_sem=sems.at[0, n], recv_sem=sems.at[1, n],
            device_id=(lax.rem(mine + 1, ncores), me), device_id_type=MESH)

    def copy_r(n):
        lanes = pl.ds(n * chunk, chunk)
        return pltpu.make_async_remote_copy(
            src_ref=sent_r.at[:, lanes], dst_ref=got_r.at[:, lanes], send_sem=sems.at[2, n], recv_sem=sems.at[3, n],
            device_id=(lax.rem(mine + ncores - 1, ncores), me), device_id_type=MESH)

    def pass_left():
        for n in range(chunks):
            c = n * chunk
            copy_l(n).wait_recv()

            def add(a, total):
                return total + got_l[pl.ds(a, 1), c:c + chunk] * mats[pl.ds(pl.multiple_of(a * R, 8), R), c:c + chunk]
            sent_l[:, c:c + chunk] = lax.fori_loop(0, R, add, jnp.zeros((R, chunk), F32), unroll=4)
            copy_l(n).start()

    def pass_right():
        for n in range(chunks):
            c = n * chunk
            copy_r(n).wait_recv()

            def one(a, _):
                m = mats[pl.ds(pl.multiple_of(a * R, 8), R), c:c + chunk] * got_r[:, c:c + chunk]
                sent_r[pl.ds(a, 1), c:c + chunk] = jnp.sum(m, axis=0, keepdims=True)
                return 0
            lax.fori_loop(0, R, one, 0, unroll=4)
            copy_r(n).start()

    @pl.when(first)
    def _():
        for n in range(chunks):
            copy_l(n).start()
        for n in range(chunks):
            copy_r(n).wait_recv()

    @pl.when(last)
    def _():
        for n in range(chunks):
            copy_r(n).start()
        for n in range(chunks):
            copy_l(n).wait_recv()

    @pl.when(jnp.logical_and(inner, 2 * mine < ncores))
    def _():
        pass_left()
        pass_right()

    @pl.when(jnp.logical_and(inner, 2 * mine >= ncores))
    def _():
        pass_right()
        pass_left()

    @pl.when(last)
    def _():
        pred[...] = jnp.sum(got_l[...] * sent_r[...], axis=0, keepdims=True)

    @pl.when(mine < ncores - 1)
    def _():
        pred[...] = jnp.sum(sent_l[...] * got_r[...], axis=0, keepdims=True)

    left_out[...] = got_l[...]
    right_out[...] = got_r[...] * (pred[...] - observed[...])
    worst = flag[...]
    for d in range(1, nsamp):
        tell(d).wait_recv()
        worst = jnp.maximum(worst, got_flag[d - 1])
    over[...] = worst
    for d in range(1, nsamp):
        tell(d).wait_send()

    @pl.when(mine < ncores - 1)
    def _():
        for n in range(chunks):
            copy_l(n).wait_send()

    @pl.when(mine > 0)
    def _():
        for n in range(chunks):
            copy_r(n).wait_send()


def against(onehot, vecs):
    nt = (((1,), (1,)), ((), ()))
    high, low = split(vecs)
    return (lax.dot_general(onehot, high, nt, preferred_element_type=F32)
            + lax.dot_general(onehot, low, nt, preferred_element_type=F32))


def edge_gradient(nsamp, onehot, left, right, rate, updated, small, got_small, kept, esend, erecv):
    mine = lax.axis_index("cores")
    me = lax.axis_index("samp")
    slab = updated.shape[0]
    at_first = (mine == 0).astype(F32)
    vec = at_first * right[...] + (1.0 - at_first) * left[...] * right[0:1, :]
    pad = jnp.zeros((128 - R, vec.shape[1]), F32)
    small[...] = against(onehot, jnp.concatenate([vec, pad], axis=0))

    def send(d):
        to = lax.rem(me + d, nsamp)
        return pltpu.make_async_remote_copy(
            src_ref=small.at[pl.ds(pl.multiple_of(to * slab, slab), slab)], dst_ref=got_small.at[d - 1],
            send_sem=esend.at[d - 1], recv_sem=erecv.at[d - 1], device_id=(mine, to), device_id_type=MESH)
    for d in range(1, nsamp):
        send(d).start()
    total = small[pl.ds(pl.multiple_of(me * slab, slab), slab), :]
    for d in range(1, nsamp):
        send(d).wait_recv()
        total = total + got_small[d - 1]
    row = lax.broadcasted_iota(jnp.int32, (128, R * R), 0)
    col = lax.broadcasted_iota(jnp.int32, (128, R * R), 1)
    stride = 1 + (R - 1) * jnp.minimum(mine, 1)
    spread = jnp.where(jnp.logical_and(col == row * stride, row < R), 1.0, 0.0).astype(BF16)
    high, low = split(total)
    updated[...] = kept[...] - rate[0, 0] * (jnp.dot(high, spread, preferred_element_type=F32)
                                             + jnp.dot(low, spread, preferred_element_type=F32))
    for d in range(1, nsamp):
        send(d).wait_send()


def gradient_kernel(ncores, nsamp, idx, left, right, cores, rate, updated, partial, got, small, got_small, kept,
                    ksem, esend, erecv, rsend, rrecv):
    mine = lax.axis_index("cores")
    me = lax.axis_index("samp")
    slab = updated.shape[0]
    half = slab // 2
    step = 8 * R
    parts = got.shape[1]
    wide = R * R // parts
    edge = jnp.logical_or(mine == 0, mine == ncores - 1)
    inner = jnp.logical_not(edge)
    barrier = pltpu.get_barrier_semaphore()
    for d in range(1, nsamp):
        pl.semaphore_signal(barrier, inc=1, device_id=(mine, lax.rem(me + d, nsamp)), device_id_type=MESH)
    keep = pltpu.make_async_copy(cores.at[0, pl.ds(pl.multiple_of(me * slab, slab), slab)], kept, ksem)
    keep.start()
    onehot = picker(idx)
    odd = lax.rem(me, 2)
    place = (1 - odd) * (me // 2) + odd * (nsamp - 1 - me // 2)

    def at_place(p):
        p = lax.rem(p + 2 * nsamp, nsamp)
        up = jnp.minimum(p // (nsamp // 2), 1)
        return (1 - up) * 2 * p + up * (2 * (nsamp - 1 - p) + 1)

    def ring(direction, c, t, peer):
        return pltpu.make_async_remote_copy(
            src_ref=got.at[direction, c, jnp.maximum(t - 1, 0)], dst_ref=got.at[direction, c, t],
            send_sem=rsend.at[direction, c, t], recv_sem=rrecv.at[direction, c, t],
            device_id=(mine, peer), device_id_type=MESH)

    def rows_of(direction, t):
        owner = at_place(place - 1 - t) if direction == 0 else at_place(place + 1 + t)
        return pl.ds(pl.multiple_of(owner * slab + direction * half, half), half)

    up_peer, down_peer = at_place(place + 1), at_place(place - 1)

    def block(t, _):
        lhs = left[pl.ds(pl.multiple_of(t * 8, 8), 8), :]
        outer = jnp.concatenate([lhs[a:a + 1, :] * right[...] for a in range(8)], axis=0)
        partial[:, pl.ds(pl.multiple_of(t * step, 128), step)] = against(onehot, outer)
        return 0

    each = R // 8 // parts

    @pl.when(inner)
    def _():
        lax.fori_loop(0, each, block, 0)

    keep.wait()
    pl.semaphore_wait(barrier, nsamp - 1)

    @pl.when(inner)
    def _():
        peers = (up_peer, down_peer)

        def begin(c):
            for direction in range(2):
                pltpu.make_async_remote_copy(
                    src_ref=partial.at[rows_of(direction, 0), pl.ds(c * wide, wide)], dst_ref=got.at[direction, c, 0],
                    send_sem=rsend.at[direction, c, 0], recv_sem=rrecv.at[direction, c, 0],
                    device_id=(mine, peers[direction]), device_id_type=MESH).start()

        def hop(c, t):
            for direction in range(2):
                ring(direction, c, t - 1, peers[direction]).wait_recv()
                got[direction, c, t - 1] = (got[direction, c, t - 1]
                                            + partial[rows_of(direction, t), c * wide:c * wide + wide])
                ring(direction, c, t, peers[direction]).start()

        def finish(c):
            end = nsamp - 2
            for direction in range(2):
                ring(direction, c, end, peers[direction]).wait_recv()
                here = (slice(direction * half, direction * half + half), slice(c * wide, c * wide + wide))
                updated[here] = kept[here] - rate[0, 0] * (
                    got[direction, c, end] + partial[rows_of(direction, end + 1), c * wide:c * wide + wide])

        for turn in range(parts):
            if turn > 0:
                lax.fori_loop(turn * each, (turn + 1) * each, block, 0)
            begin(turn)
            for c in range(turn):
                if turn - c <= nsamp - 2:
                    hop(c, turn - c)

        def steady(turn, _):
            for c in range(parts):
                hop(c, turn - c)
            return 0
        lax.fori_loop(parts, nsamp - 1, steady, 0)
        for turn in range(max(parts, nsamp - 1), parts + nsamp - 1):
            for c in range(parts):
                if turn - c <= nsamp - 2:
                    hop(c, turn - c)
                elif turn - c == nsamp - 1:
                    finish(c)

        def drain(t, _):
            for c in range(parts):
                for direction in range(2):
                    ring(direction, c, t, peers[direction]).wait_send()
            return 0
        lax.fori_loop(0, nsamp - 1, drain, 0)

    @pl.when(edge)
    def _():
        edge_gradient(nsamp, onehot, left, right, rate, updated, small, got_small, kept, esend, erecv)


def routed_kernel(ncores, nsamp, room, idx, left, right, cores, rate, updated, packed, got, small, got_small, kept,
                  ksem, esend, erecv, psend, precv):
    mine = lax.axis_index("cores")
    me = lax.axis_index("samp")
    count = idx.shape[1]
    slab = updated.shape[0]
    edge = jnp.logical_or(mine == 0, mine == ncores - 1)
    barrier = pltpu.get_barrier_semaphore()
    for d in range(1, nsamp):
        pl.semaphore_signal(barrier, inc=1, device_id=(mine, lax.rem(me + d, nsamp)), device_id_type=MESH)
    keep = pltpu.make_async_copy(cores.at[0, pl.ds(pl.multiple_of(me * slab, slab), slab)], kept, ksem)
    keep.start()

    @pl.when(edge)
    def _():
        keep.wait()
        pl.semaphore_wait(barrier, nsamp - 1)
        edge_gradient(nsamp, picker(idx), left, right, rate, updated, small, got_small, kept, esend, erecv)

    @pl.when(jnp.logical_not(edge))
    def _():
        slab_of = idx[...] // slab
        member = jnp.where(lax.broadcasted_iota(jnp.int32, (16, count), 0) == slab_of, 1.0, 0.0)
        before = jnp.where(lax.broadcasted_iota(jnp.int32, (count, count), 0)
                           < lax.broadcasted_iota(jnp.int32, (count, count), 1), 1.0, 0.0).astype(BF16)
        earlier = jnp.dot(member.astype(BF16), before, preferred_element_type=F32)
        place = slab_of * room + jnp.sum(member * earlier, axis=0, keepdims=True).astype(jnp.int32)
        high, low = split(jnp.concatenate([left[...], right[...]], axis=0))
        within = jnp.broadcast_to((idx[...] - slab_of * slab).astype(F32), (16, count)).astype(BF16)
        rows = jnp.concatenate([high, low, within], axis=0)
        spot = lax.broadcasted_iota(jnp.int32, (room, count), 0)

        def send(d):
            return pltpu.make_async_remote_copy(
                src_ref=packed.at[d], dst_ref=got.at[d], send_sem=psend.at[d], recv_sem=precv.at[d],
                device_id=(mine, lax.rem(me + d, nsamp)), device_id_type=MESH)

        def pack(d):
            to = lax.rem(me + d, nsamp)
            pick = jnp.where(spot == place - to * room, 1.0, 0.0).astype(BF16)
            out = lax.dot_general(rows, pick, (((1,), (1,)), ((), ())), preferred_element_type=F32)
            return jnp.concatenate([out[:2 * R] + out[2 * R:4 * R], out[4 * R:4 * R + 8]], axis=0)

        def dispatch(d, _):
            packed[d] = pack(d)

            @pl.when(d == 1)
            def _():
                pl.semaphore_wait(barrier, nsamp - 1)
            send(d).start()
            return 0
        lax.fori_loop(1, nsamp, dispatch, 0)
        got[0] = pack(0)
        keep.wait()
        group = count // room
        step = 16 * R
        for g in range(0, nsamp, group):
            for d in range(max(g, 1), g + group):
                send(d).wait_recv()
            vecs = jnp.concatenate([got[d] for d in range(g, g + group)], axis=1)
            ids = vecs[2 * R:2 * R + 1].astype(jnp.int32)
            slices = jnp.where(lax.broadcasted_iota(jnp.int32, (slab, count), 0) == ids, 1.0, 0.0).astype(BF16)
            for t in range(0, R, 16):
                outer = jnp.concatenate([vecs[a:a + 1] * vecs[R:2 * R] for a in range(t, t + 16)], axis=0)
                here = slice(t * R, t * R + step)
                base = kept[:, here] if g == 0 else updated[:, here]
                updated[:, here] = base - rate[0, 0] * against(slices, outer)
        for d in range(1, nsamp):
            send(d).wait_send()


def eliminate(mats):
    row = lax.broadcasted_iota(jnp.int32, (R, 128), 0)
    lane = lax.broadcasted_iota(jnp.int32, (R, 128), 1)
    mats = [jnp.concatenate([m, (row == lane).astype(F32)[:, :W]], axis=1) for m in mats]
    for j in range(0, R, 2):
        nxt = []
        for m in mats:
            col0 = jnp.broadcast_to(m[:, j:j + 1], (R, 128))
            col1 = jnp.broadcast_to(m[:, j + 1:j + 2], (R, 128))
            inv0 = 1.0 / col0[j:j + 1]
            ratio = col0[j + 1:j + 2] * inv0
            inv1 = 1.0 / (col1[j + 1:j + 2] - ratio * col0[j + 1:j + 2])
            row0 = m[j:j + 1]
            row1 = m[j + 1:j + 2] - ratio * row0
            col1 = jnp.where(row > j + 1, col1 - col0 * ratio, 0.0)
            col0 = jnp.where(row > j, col0, 0.0)
            nxt.append(m - col0 * (row0 * inv0) - col1 * (row1 * inv1))
        mats = nxt
    outs = []
    for m in mats:
        diag = jnp.sum(jnp.where(row == lane, m, 0.0), axis=1, keepdims=True)
        outs.append(m * lax.rsqrt(diag))
    return outs


def finish_kernel(pairs, uwide, hprev, hown, out):
    first, second = eliminate([hprev[...], hown[...]])
    carry = first[:, :W]
    inv = second[:, W:]
    tall = tall_of(weigh(carry, three(uwide[...])), pairs)
    pad = jnp.zeros((W - R, W), F32)
    inv = jnp.concatenate([inv, pad], axis=0)
    zero = jnp.zeros((W, W), F32)
    diag = jnp.concatenate([jnp.concatenate([inv, zero], axis=1), jnp.concatenate([zero, inv], axis=1)], axis=0)
    out[...] = lax.dot_general(tall, diag, (((1,), (1,)), ((), ())), precision=HIGH, preferred_element_type=F32)


def retract(updated, ncores, nsamp):
    slab = updated.shape[0]
    pairs = slab // 2
    vm = pl.BlockSpec(memory_space=pltpu.VMEM)
    uwide = jnp.pad(updated.reshape(slab, R, R).transpose(1, 0, 2), ((0, W - R), (0, 0), (0, W - R)))
    uwide = uwide.reshape(W, slab * W)
    square = jax.ShapeDtypeStruct((R, W), F32)
    hprev, hown = pl.pallas_call(
        functools.partial(gram_kernel, ncores, nsamp, pairs),
        out_shape=(square, square),
        in_specs=[vm],
        out_specs=(vm, vm),
        scratch_shapes=[
            pltpu.VMEM((R // 2, 128), F32),
            pltpu.VMEM((nsamp, R // 2, 128), F32),
            pltpu.VMEM((nsamp - 1, R // 2, 128), F32),
            pltpu.SemaphoreType.DMA((nsamp - 1,)),
            pltpu.SemaphoreType.DMA((nsamp,)),
            pltpu.SemaphoreType.DMA((nsamp - 1,)),
            pltpu.SemaphoreType.DMA((nsamp,)),
        ],
        compiler_params=pltpu.CompilerParams(collective_id=0, has_side_effects=True, vmem_limit_bytes=32 << 20),
        name="gram_chain",
    )(uwide)
    tall = pl.pallas_call(
        functools.partial(finish_kernel, pairs),
        out_shape=jax.ShapeDtypeStruct((pairs * R, 128), F32),
        in_specs=[vm] * 3,
        out_specs=vm,
        compiler_params=pltpu.CompilerParams(vmem_limit_bytes=32 << 20),
        name="finish",
    )(uwide, hprev, hown)
    tall = tall.reshape(pairs, R, 2, W)[..., :R]
    return tall.transpose(0, 2, 1, 3).reshape(slab, R * R)


def on_device(cores, indices, observed, step_size):
    ncores = lax.axis_size("cores")
    mine = lax.axis_index("cores")
    nsamp = lax.axis_size("samp")
    count = indices.shape[0]
    own_index = lax.dynamic_index_in_dim(indices, mine, 1, keepdims=False)
    slab = N // nsamp
    parts = 3
    room = max(2 * count // nsamp, 128)
    vm = pl.BlockSpec(memory_space=pltpu.VMEM)
    vectors = jax.ShapeDtypeStruct((R, count), F32)
    left, right, over = pl.pallas_call(
        functools.partial(front_kernel, ncores, nsamp, room),
        out_shape=(vectors, vectors, jax.ShapeDtypeStruct((8, 128), F32)),
        in_specs=[pl.BlockSpec(memory_space=pl.ANY), vm, vm, vm],
        out_specs=(vm, vm, vm),
        scratch_shapes=[
            pltpu.VMEM((N, R * R), F32),
            pltpu.VMEM((R * R, count), F32),
            pltpu.VMEM((R, count), F32),
            pltpu.VMEM((R, count), F32),
            pltpu.VMEM((R, count), F32),
            pltpu.VMEM((R, count), F32),
            pltpu.VMEM((1, count), F32),
            pltpu.VMEM((8, 128), F32),
            pltpu.VMEM((nsamp - 1, 8, 128), F32),
            pltpu.SemaphoreType.DMA((R // 8,)),
            pltpu.SemaphoreType.DMA((4, count // 256)),
            pltpu.SemaphoreType.DMA((nsamp - 1,)),
            pltpu.SemaphoreType.DMA((nsamp - 1,)),
        ],
        compiler_params=pltpu.CompilerParams(collective_id=1, has_side_effects=True, vmem_limit_bytes=48 << 20),
        name="sample_vectors",
    )(cores, own_index.reshape(1, count), indices.T, observed.reshape(1, count))
    summed = pl.pallas_call(
        functools.partial(gradient_kernel, ncores, nsamp),
        out_shape=jax.ShapeDtypeStruct((slab, R * R), F32),
        in_specs=[vm] * 3 + [pl.BlockSpec(memory_space=pl.ANY), pl.BlockSpec(memory_space=pltpu.SMEM)],
        out_specs=vm,
        scratch_shapes=[
            pltpu.VMEM((N, R * R), F32),
            pltpu.VMEM((2, parts, nsamp - 1, slab // 2, R * R // parts), F32),
            pltpu.VMEM((N, 128), F32),
            pltpu.VMEM((nsamp - 1, slab, 128), F32),
            pltpu.VMEM((slab, R * R), F32),
            pltpu.SemaphoreType.DMA,
            pltpu.SemaphoreType.DMA((nsamp - 1,)),
            pltpu.SemaphoreType.DMA((nsamp - 1,)),
            pltpu.SemaphoreType.DMA((2, parts, nsamp - 1)),
            pltpu.SemaphoreType.DMA((2, parts, nsamp - 1)),
        ],
        compiler_params=pltpu.CompilerParams(collective_id=2, has_side_effects=True, vmem_limit_bytes=48 << 20),
        name="gradient_sum",
    )
    routed = pl.pallas_call(
        functools.partial(routed_kernel, ncores, nsamp, room),
        out_shape=jax.ShapeDtypeStruct((slab, R * R), F32),
        in_specs=[vm] * 3 + [pl.BlockSpec(memory_space=pl.ANY), pl.BlockSpec(memory_space=pltpu.SMEM)],
        out_specs=vm,
        scratch_shapes=[
            pltpu.VMEM((nsamp, 2 * R + 8, room), F32),
            pltpu.VMEM((nsamp, 2 * R + 8, room), F32),
            pltpu.VMEM((N, 128), F32),
            pltpu.VMEM((nsamp - 1, slab, 128), F32),
            pltpu.VMEM((slab, R * R), F32),
            pltpu.SemaphoreType.DMA,
            pltpu.SemaphoreType.DMA((nsamp - 1,)),
            pltpu.SemaphoreType.DMA((nsamp - 1,)),
            pltpu.SemaphoreType.DMA((nsamp,)),
            pltpu.SemaphoreType.DMA((nsamp,)),
        ],
        compiler_params=pltpu.CompilerParams(collective_id=3, has_side_effects=True, vmem_limit_bytes=48 << 20),
        name="gradient_routed",
    )
    updated = lax.cond(over[0, 0] == 0.0, routed, summed,
                       own_index.reshape(1, count), left, right, cores, step_size.reshape(1, 1))
    return retract(updated, ncores, nsamp)[None]


def solution(mesh):
    in_specs = (P("cores", None, None), P("samp", None), P("samp"), P())
    out_specs = P("cores", "samp", None)
    return jax.shard_map(
        on_device, mesh=mesh, in_specs=in_specs, out_specs=out_specs, check_vma=False
    )
```

```python
import functools

import jax
import jax.numpy as jnp
from jax import lax
from jax.experimental import pallas as pl
from jax.experimental.pallas import tpu as pltpu
from jax.sharding import PartitionSpec as P

R = 48
N = 512
W = 64

HIGH = lax.Precision.HIGHEST
MESH = pl.DeviceIdType.MESH
F32 = jnp.float32
BF16 = jnp.bfloat16


def split(x):
    high = x.astype(BF16)
    low = (x - high.astype(F32)).astype(BF16)
    return high, low


def three(x):
    high, low = split(x)
    return jnp.concatenate([high, low, high], axis=0)


def weigh(mat, ustack):
    high, low = split(mat)
    return jnp.dot(jnp.concatenate([high, high, low], axis=1), ustack, preferred_element_type=F32)


def padded(x):
    return jnp.concatenate([x, jnp.zeros((W - x.shape[0], x.shape[1]), F32)], axis=0)


def across(ref, width):
    return jnp.concatenate([ref[pl.ds(n, R, stride=R), :][:, :width] for n in range(R)], axis=1)


def along(ref, width):
    return jnp.concatenate([ref[R * n:R * n + R, :][:, :width] for n in range(R)], axis=1)


def lay(ref, wide, width):
    for n in range(R):
        ref[R * n:R * n + R, 0:width] = wide[:, n * width:n * width + width]


def greet_modes(barrier):
    mine = lax.axis_index("cores")

    @pl.when(mine > 0)
    def _():
        pl.semaphore_signal(barrier, inc=1, device_id=(mine - 1, lax.axis_index("samp")), device_id_type=MESH)


def chain(ncores, nsamp, updated, hprev, hown, turned, moved, sendbuf, total_buf, got_prev, got_own,
          send_own, recv_own, hop_sems):
    mine = lax.axis_index("cores")
    me = lax.axis_index("samp")
    slab = updated.shape[0]
    has_prev = mine > 0
    has_next = mine < ncores - 1

    def own_copy(d):
        return pltpu.make_async_remote_copy(
            src_ref=sendbuf, dst_ref=got_own.at[d - 1], send_sem=send_own.at[d - 1],
            recv_sem=recv_own.at[d - 1], device_id=(mine, lax.rem(me + d, nsamp)), device_id_type=MESH)

    onward = pltpu.make_async_remote_copy(
        src_ref=total_buf, dst_ref=got_prev, send_sem=hop_sems.at[0], recv_sem=hop_sems.at[1],
        device_id=(lax.rem(mine + 1, ncores), me), device_id_type=MESH)

    def unpack(x):
        return jnp.concatenate([x[:, :W], x[:, W:]], axis=0)

    row = lax.broadcasted_iota(jnp.int32, (R, W), 0)
    lane = lax.broadcasted_iota(jnp.int32, (R, W), 1)
    eye = (row == lane).astype(F32)
    hprev[...] = eye
    hown[...] = eye

    @pl.when(has_next)
    def _():
        turned[:, 0:slab] = updated[...].T
        ustack = three(padded(across(turned, slab)))
        zh, zl = split(along(turned, slab))

        @pl.when(has_prev)
        def _():
            onward.wait_recv()
            hprev[...] = unpack(got_prev[...])

        lay(moved, weigh(hprev[...], ustack), slab)
        yh, yl = split(across(moved, slab))
        nt = (((1,), (1,)), ((), ()))
        gram = lax.dot_general(zh, yh, nt, preferred_element_type=F32)
        gram = gram + lax.dot_general(zh, yl, nt, preferred_element_type=F32)
        gram = gram + lax.dot_general(zl, yh, nt, preferred_element_type=F32)
        gram = jnp.concatenate([gram * (1.0 / N), jnp.zeros((R, W - R), F32)], axis=1)
        sendbuf[...] = jnp.concatenate([gram[:R // 2], gram[R // 2:]], axis=1)
        for d in range(1, nsamp):
            own_copy(d).start()
        total = sendbuf[...]
        for d in range(1, nsamp):
            own_copy(d).wait_recv()
            total = total + got_own[d - 1]
        total_buf[...] = total
        onward.start()
        hown[...] = unpack(total)
        for d in range(1, nsamp):
            own_copy(d).wait_send()
        onward.wait_send()

    @pl.when(jnp.logical_not(has_next))
    def _():
        onward.wait_recv()
        hprev[...] = unpack(got_prev[...])


def picker(idx_ref):
    count = idx_ref.shape[1]
    row = lax.broadcasted_iota(jnp.int32, (N, count), 0)
    return jnp.where(row == idx_ref[...], 1.0, 0.0).astype(BF16)


def front_kernel(ncores, nsamp, room, cores, idx, every, observed, left_out, right_out, over, table, mats, sent_l, sent_r, got_l, got_r, pred,
                 flag, got_flag, loads, sems, fsend, frecv):
    mine = lax.axis_index("cores")
    me = lax.axis_index("samp")
    count = idx.shape[1]
    step = 8 * R
    blocks = R // 8
    chunk = 256
    chunks = count // chunk
    first, last = mine == 0, mine == ncores - 1
    inner = jnp.logical_not(jnp.logical_or(first, last))
    barrier = pltpu.get_barrier_semaphore()

    def load(t):
        lanes = pl.ds(pl.multiple_of(t * step, 128), step)
        return pltpu.make_async_copy(cores.at[0, :, lanes], table.at[:, lanes], loads.at[t])

    for t in range(blocks):
        load(t).start()

    @pl.when(mine > 0)
    def _():
        pl.semaphore_signal(barrier, inc=1, device_id=(mine - 1, me), device_id_type=MESH)

    @pl.when(mine < ncores - 1)
    def _():
        pl.semaphore_signal(barrier, inc=1, device_id=(mine + 1, me), device_id_type=MESH)

    for d in range(1, nsamp):
        pl.semaphore_signal(barrier, inc=1, device_id=(mine, lax.rem(me + d, nsamp)), device_id_type=MESH)

    def tell(d):
        return pltpu.make_async_remote_copy(
            src_ref=flag, dst_ref=got_flag.at[d - 1], send_sem=fsend.at[d - 1], recv_sem=frecv.at[d - 1],
            device_id=(mine, lax.rem(me + d, nsamp)), device_id_type=MESH)

    most = jnp.zeros((nsamp, 1), F32)
    owner = lax.broadcasted_iota(jnp.int32, (nsamp, count), 0)
    for m in range(ncores):
        member = jnp.where(every[m:m + 1, :] // (N // nsamp) == owner, 1.0, 0.0)
        most = jnp.maximum(most, jnp.sum(member, axis=1, keepdims=True))
    most = jnp.max(most, axis=0, keepdims=True)
    flag[...] = jnp.broadcast_to(jnp.where(most > room, 1.0, 0.0), (8, 128))

    onehot = picker(idx)
    unit = (lax.broadcasted_iota(jnp.int32, (R, count), 0) == 0).astype(F32)

    def picked(part):
        high, low = split(part.T)
        return (jnp.dot(high, onehot, preferred_element_type=F32)
                + jnp.dot(low, onehot, preferred_element_type=F32))

    @pl.when(first)
    def _():
        load(0).wait()
        sent_l[...] = picked(table[:, 0:128])[0:R]
        got_l[...] = unit
        for t in range(1, blocks):
            load(t).wait()

    @pl.when(last)
    def _():
        for t in range(blocks):
            load(t).wait()
        row = lax.broadcasted_iota(jnp.int32, (R * R, 128), 0)
        col = lax.broadcasted_iota(jnp.int32, (R * R, 128), 1)
        heads = jnp.where(jnp.logical_and(row == col * R, col < R), 1.0, 0.0).astype(BF16)
        high, low = split(table[...])
        part = jnp.dot(high, heads, preferred_element_type=F32) + jnp.dot(low, heads, preferred_element_type=F32)
        sent_r[...] = picked(part)[0:R]
        got_r[...] = unit

    @pl.when(inner)
    def _():
        def fill(t, _):
            load(t).wait()
            at = pl.multiple_of(t * step, step)
            mats[pl.ds(at, step), :] = picked(table[:, pl.ds(at, step)])
            return 0
        lax.fori_loop(0, blocks, fill, 0)

    pl.semaphore_wait(barrier, nsamp - 1 + jnp.minimum(mine, 1) + jnp.minimum(ncores - 1 - mine, 1))
    for d in range(1, nsamp):
        tell(d).start()

    def copy_l(n):
        lanes = pl.ds(n * chunk, chunk)
        return pltpu.make_async_remote_copy(
            src_ref=sent_l.at[:, lanes], dst_ref=got_l.at[:, lanes], send_sem=sems.at[0, n], recv_sem=sems.at[1, n],
            device_id=(lax.rem(mine + 1, ncores), me), device_id_type=MESH)

    def copy_r(n):
        lanes = pl.ds(n * chunk, chunk)
        return pltpu.make_async_remote_copy(
            src_ref=sent_r.at[:, lanes], dst_ref=got_r.at[:, lanes], send_sem=sems.at[2, n], recv_sem=sems.at[3, n],
            device_id=(lax.rem(mine + ncores - 1, ncores), me), device_id_type=MESH)

    def pass_left():
        for n in range(chunks):
            c = n * chunk
            copy_l(n).wait_recv()

            def add(a, total):
                return total + got_l[pl.ds(a, 1), c:c + chunk] * mats[pl.ds(pl.multiple_of(a * R, 8), R), c:c + chunk]
            sent_l[:, c:c + chunk] = lax.fori_loop(0, R, add, jnp.zeros((R, chunk), F32), unroll=4)
            copy_l(n).start()

    def pass_right():
        for n in range(chunks):
            c = n * chunk
            copy_r(n).wait_recv()

            def one(a, _):
                m = mats[pl.ds(pl.multiple_of(a * R, 8), R), c:c + chunk] * got_r[:, c:c + chunk]
                sent_r[pl.ds(a, 1), c:c + chunk] = jnp.sum(m, axis=0, keepdims=True)
                return 0
            lax.fori_loop(0, R, one, 0, unroll=4)
            copy_r(n).start()

    @pl.when(first)
    def _():
        for n in range(chunks):
            copy_l(n).start()
        for n in range(chunks):
            copy_r(n).wait_recv()

    @pl.when(last)
    def _():
        for n in range(chunks):
            copy_r(n).start()
        for n in range(chunks):
            copy_l(n).wait_recv()

    @pl.when(jnp.logical_and(inner, 2 * mine < ncores))
    def _():
        pass_left()
        pass_right()

    @pl.when(jnp.logical_and(inner, 2 * mine >= ncores))
    def _():
        pass_right()
        pass_left()

    @pl.when(last)
    def _():
        pred[...] = jnp.sum(got_l[...] * sent_r[...], axis=0, keepdims=True)

    @pl.when(mine < ncores - 1)
    def _():
        pred[...] = jnp.sum(sent_l[...] * got_r[...], axis=0, keepdims=True)

    left_out[...] = got_l[...]
    right_out[...] = got_r[...] * (pred[...] - observed[...])
    worst = flag[...]
    for d in range(1, nsamp):
        tell(d).wait_recv()
        worst = jnp.maximum(worst, got_flag[d - 1])
    over[...] = worst
    for d in range(1, nsamp):
        tell(d).wait_send()

    @pl.when(mine < ncores - 1)
    def _():
        for n in range(chunks):
            copy_l(n).wait_send()

    @pl.when(mine > 0)
    def _():
        for n in range(chunks):
            copy_r(n).wait_send()


def against(onehot, vecs):
    nt = (((1,), (1,)), ((), ()))
    high, low = split(vecs)
    return (lax.dot_general(onehot, high, nt, preferred_element_type=F32)
            + lax.dot_general(onehot, low, nt, preferred_element_type=F32))


def edge_gradient(nsamp, onehot, left, right, rate, updated, small, got_small, kept, esend, erecv):
    mine = lax.axis_index("cores")
    me = lax.axis_index("samp")
    slab = updated.shape[0]
    at_first = (mine == 0).astype(F32)
    vec = at_first * right[...] + (1.0 - at_first) * left[...] * right[0:1, :]
    pad = jnp.zeros((128 - R, vec.shape[1]), F32)
    small[...] = against(onehot, jnp.concatenate([vec, pad], axis=0))

    def send(d):
        to = lax.rem(me + d, nsamp)
        return pltpu.make_async_remote_copy(
            src_ref=small.at[pl.ds(pl.multiple_of(to * slab, slab), slab)], dst_ref=got_small.at[d - 1],
            send_sem=esend.at[d - 1], recv_sem=erecv.at[d - 1], device_id=(mine, to), device_id_type=MESH)
    for d in range(1, nsamp):
        send(d).start()
    total = small[pl.ds(pl.multiple_of(me * slab, slab), slab), :]
    for d in range(1, nsamp):
        send(d).wait_recv()
        total = total + got_small[d - 1]
    row = lax.broadcasted_iota(jnp.int32, (128, R * R), 0)
    col = lax.broadcasted_iota(jnp.int32, (128, R * R), 1)
    stride = 1 + (R - 1) * jnp.minimum(mine, 1)
    spread = jnp.where(jnp.logical_and(col == row * stride, row < R), 1.0, 0.0).astype(BF16)
    high, low = split(total)
    updated[...] = kept[...] - rate[0, 0] * (jnp.dot(high, spread, preferred_element_type=F32)
                                             + jnp.dot(low, spread, preferred_element_type=F32))
    for d in range(1, nsamp):
        send(d).wait_send()


def gradient_kernel(ncores, nsamp, idx, left, right, cores, rate, updated, hprev, hown, partial, got, small, got_small, kept,
                    ksem, esend, erecv, rsend, rrecv, *links):
    mine = lax.axis_index("cores")
    me = lax.axis_index("samp")
    slab = updated.shape[0]
    half = slab // 2
    step = 8 * R
    parts = got.shape[1]
    wide = R * R // parts
    edge = jnp.logical_or(mine == 0, mine == ncores - 1)
    inner = jnp.logical_not(edge)
    barrier = pltpu.get_barrier_semaphore()
    for d in range(1, nsamp):
        pl.semaphore_signal(barrier, inc=1, device_id=(mine, lax.rem(me + d, nsamp)), device_id_type=MESH)
    greet_modes(barrier)
    keep = pltpu.make_async_copy(cores.at[0, pl.ds(pl.multiple_of(me * slab, slab), slab)], kept, ksem)
    keep.start()
    onehot = picker(idx)
    odd = lax.rem(me, 2)
    place = (1 - odd) * (me // 2) + odd * (nsamp - 1 - me // 2)

    def at_place(p):
        p = lax.rem(p + 2 * nsamp, nsamp)
        up = jnp.minimum(p // (nsamp // 2), 1)
        return (1 - up) * 2 * p + up * (2 * (nsamp - 1 - p) + 1)

    def ring(direction, c, t, peer):
        return pltpu.make_async_remote_copy(
            src_ref=got.at[direction, c, jnp.maximum(t - 1, 0)], dst_ref=got.at[direction, c, t],
            send_sem=rsend.at[direction, c, t], recv_sem=rrecv.at[direction, c, t],
            device_id=(mine, peer), device_id_type=MESH)

    def rows_of(direction, t):
        owner = at_place(place - 1 - t) if direction == 0 else at_place(place + 1 + t)
        return pl.ds(pl.multiple_of(owner * slab + direction * half, half), half)

    up_peer, down_peer = at_place(place + 1), at_place(place - 1)

    def block(t, _):
        lhs = left[pl.ds(pl.multiple_of(t * 8, 8), 8), :]
        outer = jnp.concatenate([lhs[a:a + 1, :] * right[...] for a in range(8)], axis=0)
        partial[:, pl.ds(pl.multiple_of(t * step, 128), step)] = against(onehot, outer)
        return 0

    each = R // 8 // parts

    @pl.when(inner)
    def _():
        lax.fori_loop(0, each, block, 0)

    keep.wait()
    pl.semaphore_wait(barrier, nsamp - 1 + jnp.minimum(ncores - 1 - mine, 1))

    @pl.when(inner)
    def _():
        peers = (up_peer, down_peer)

        def begin(c):
            for direction in range(2):
                pltpu.make_async_remote_copy(
                    src_ref=partial.at[rows_of(direction, 0), pl.ds(c * wide, wide)], dst_ref=got.at[direction, c, 0],
                    send_sem=rsend.at[direction, c, 0], recv_sem=rrecv.at[direction, c, 0],
                    device_id=(mine, peers[direction]), device_id_type=MESH).start()

        def hop(c, t):
            for direction in range(2):
                ring(direction, c, t - 1, peers[direction]).wait_recv()
                got[direction, c, t - 1] = (got[direction, c, t - 1]
                                            + partial[rows_of(direction, t), c * wide:c * wide + wide])
                ring(direction, c, t, peers[direction]).start()

        def finish(c):
            end = nsamp - 2
            for direction in range(2):
                ring(direction, c, end, peers[direction]).wait_recv()
                here = (slice(direction * half, direction * half + half), slice(c * wide, c * wide + wide))
                updated[here] = kept[here] - rate[0, 0] * (
                    got[direction, c, end] + partial[rows_of(direction, end + 1), c * wide:c * wide + wide])

        for turn in range(parts):
            if turn > 0:
                lax.fori_loop(turn * each, (turn + 1) * each, block, 0)
            begin(turn)
            for c in range(turn):
                if turn - c <= nsamp - 2:
                    hop(c, turn - c)

        def steady(turn, _):
            for c in range(parts):
                hop(c, turn - c)
            return 0
        lax.fori_loop(parts, nsamp - 1, steady, 0)
        for turn in range(max(parts, nsamp - 1), parts + nsamp - 1):
            for c in range(parts):
                if turn - c <= nsamp - 2:
                    hop(c, turn - c)
                elif turn - c == nsamp - 1:
                    finish(c)

        def drain(t, _):
            for c in range(parts):
                for direction in range(2):
                    ring(direction, c, t, peers[direction]).wait_send()
            return 0
        lax.fori_loop(0, nsamp - 1, drain, 0)

    @pl.when(edge)
    def _():
        edge_gradient(nsamp, onehot, left, right, rate, updated, small, got_small, kept, esend, erecv)

    chain(ncores, nsamp, updated, hprev, hown, *links)


def routed_kernel(ncores, nsamp, room, idx, left, right, cores, rate, updated, hprev, hown, packed, got, small, got_small, kept,
                  ksem, esend, erecv, psend, precv, *links):
    mine = lax.axis_index("cores")
    me = lax.axis_index("samp")
    count = idx.shape[1]
    slab = updated.shape[0]
    edge = jnp.logical_or(mine == 0, mine == ncores - 1)
    barrier = pltpu.get_barrier_semaphore()
    for d in range(1, nsamp):
        pl.semaphore_signal(barrier, inc=1, device_id=(mine, lax.rem(me + d, nsamp)), device_id_type=MESH)
    greet_modes(barrier)
    keep = pltpu.make_async_copy(cores.at[0, pl.ds(pl.multiple_of(me * slab, slab), slab)], kept, ksem)
    keep.start()

    @pl.when(edge)
    def _():
        keep.wait()
        pl.semaphore_wait(barrier, nsamp - 1 + jnp.minimum(ncores - 1 - mine, 1))
        edge_gradient(nsamp, picker(idx), left, right, rate, updated, small, got_small, kept, esend, erecv)

    @pl.when(jnp.logical_not(edge))
    def _():
        slab_of = idx[...] // slab
        member = jnp.where(lax.broadcasted_iota(jnp.int32, (16, count), 0) == slab_of, 1.0, 0.0)
        before = jnp.where(lax.broadcasted_iota(jnp.int32, (count, count), 0)
                           < lax.broadcasted_iota(jnp.int32, (count, count), 1), 1.0, 0.0).astype(BF16)
        earlier = jnp.dot(member.astype(BF16), before, preferred_element_type=F32)
        place = slab_of * room + jnp.sum(member * earlier, axis=0, keepdims=True).astype(jnp.int32)
        high, low = split(jnp.concatenate([left[...], right[...]], axis=0))
        within = jnp.broadcast_to((idx[...] - slab_of * slab).astype(F32), (16, count)).astype(BF16)
        rows = jnp.concatenate([high, low, within], axis=0)
        spot = lax.broadcasted_iota(jnp.int32, (room, count), 0)

        def send(d):
            return pltpu.make_async_remote_copy(
                src_ref=packed.at[d], dst_ref=got.at[d], send_sem=psend.at[d], recv_sem=precv.at[d],
                device_id=(mine, lax.rem(me + d, nsamp)), device_id_type=MESH)

        def pack(d):
            to = lax.rem(me + d, nsamp)
            pick = jnp.where(spot == place - to * room, 1.0, 0.0).astype(BF16)
            out = lax.dot_general(rows, pick, (((1,), (1,)), ((), ())), preferred_element_type=F32)
            return jnp.concatenate([out[:2 * R] + out[2 * R:4 * R], out[4 * R:4 * R + 8]], axis=0)

        def dispatch(d, _):
            packed[d] = pack(d)

            @pl.when(d == 1)
            def _():
                pl.semaphore_wait(barrier, nsamp - 1 + jnp.minimum(ncores - 1 - mine, 1))
            send(d).start()
            return 0
        lax.fori_loop(1, nsamp, dispatch, 0)
        got[0] = pack(0)
        keep.wait()
        group = count // room
        step = 16 * R
        for g in range(0, nsamp, group):
            for d in range(max(g, 1), g + group):
                send(d).wait_recv()
            vecs = jnp.concatenate([got[d] for d in range(g, g + group)], axis=1)
            ids = vecs[2 * R:2 * R + 1].astype(jnp.int32)
            slices = jnp.where(lax.broadcasted_iota(jnp.int32, (slab, count), 0) == ids, 1.0, 0.0).astype(BF16)
            for t in range(0, R, 16):
                outer = jnp.concatenate([vecs[a:a + 1] * vecs[R:2 * R] for a in range(t, t + 16)], axis=0)
                here = slice(t * R, t * R + step)
                base = kept[:, here] if g == 0 else updated[:, here]
                updated[:, here] = base - rate[0, 0] * against(slices, outer)
        for d in range(1, nsamp):
            send(d).wait_send()

    chain(ncores, nsamp, updated, hprev, hown, *links)


def eliminate(mats):
    row = lax.broadcasted_iota(jnp.int32, (R, 128), 0)
    lane = lax.broadcasted_iota(jnp.int32, (R, 128), 1)
    mats = [jnp.concatenate([m, (row == lane).astype(F32)[:, :W]], axis=1) for m in mats]
    for j in range(0, R, 2):
        nxt = []
        for m in mats:
            col0 = jnp.broadcast_to(m[:, j:j + 1], (R, 128))
            col1 = jnp.broadcast_to(m[:, j + 1:j + 2], (R, 128))
            inv0 = 1.0 / col0[j:j + 1]
            ratio = col0[j + 1:j + 2] * inv0
            inv1 = 1.0 / (col1[j + 1:j + 2] - ratio * col0[j + 1:j + 2])
            row0 = m[j:j + 1]
            row1 = m[j + 1:j + 2] - ratio * row0
            col1 = jnp.where(row > j + 1, col1 - col0 * ratio, 0.0)
            col0 = jnp.where(row > j, col0, 0.0)
            nxt.append(m - col0 * (row0 * inv0) - col1 * (row1 * inv1))
        mats = nxt
    outs = []
    for m in mats:
        diag = jnp.sum(jnp.where(row == lane, m, 0.0), axis=1, keepdims=True)
        outs.append(m * lax.rsqrt(diag))
    return outs


def finish_kernel(updated, hprev, hown, out, turned, moved):
    slab = updated.shape[0]
    turned[:, 0:slab] = updated[...].T
    ustack = three(padded(across(turned, slab)))
    first, second = eliminate([hprev[...], hown[...]])
    lay(moved, weigh(first[:, :W], ustack), slab)
    ystack = three(padded(across(moved, slab)))
    lay(turned, weigh(second[:, W:], ystack), slab)
    out[...] = turned[:, 0:slab].T


def on_device(cores, indices, observed, step_size):
    ncores = lax.axis_size("cores")
    mine = lax.axis_index("cores")
    nsamp = lax.axis_size("samp")
    count = indices.shape[0]
    own_index = lax.dynamic_index_in_dim(indices, mine, 1, keepdims=False)
    slab = N // nsamp
    parts = 3
    room = max(2 * count // nsamp, 128)
    vm = pl.BlockSpec(memory_space=pltpu.VMEM)
    vectors = jax.ShapeDtypeStruct((R, count), F32)
    left, right, over = pl.pallas_call(
        functools.partial(front_kernel, ncores, nsamp, room),
        out_shape=(vectors, vectors, jax.ShapeDtypeStruct((8, 128), F32)),
        in_specs=[pl.BlockSpec(memory_space=pl.ANY), vm, vm, vm],
        out_specs=(vm, vm, vm),
        scratch_shapes=[
            pltpu.VMEM((N, R * R), F32),
            pltpu.VMEM((R * R, count), F32),
            pltpu.VMEM((R, count), F32),
            pltpu.VMEM((R, count), F32),
            pltpu.VMEM((R, count), F32),
            pltpu.VMEM((R, count), F32),
            pltpu.VMEM((1, count), F32),
            pltpu.VMEM((8, 128), F32),
            pltpu.VMEM((nsamp - 1, 8, 128), F32),
            pltpu.SemaphoreType.DMA((R // 8,)),
            pltpu.SemaphoreType.DMA((4, count // 256)),
            pltpu.SemaphoreType.DMA((nsamp - 1,)),
            pltpu.SemaphoreType.DMA((nsamp - 1,)),
        ],
        compiler_params=pltpu.CompilerParams(collective_id=1, has_side_effects=True, vmem_limit_bytes=48 << 20),
        name="sample_vectors",
    )(cores, own_index.reshape(1, count), indices.T, observed.reshape(1, count))
    new_slices = jax.ShapeDtypeStruct((slab, R * R), F32)
    square = jax.ShapeDtypeStruct((R, W), F32)
    half = pltpu.VMEM((R // 2, 128), F32)
    turning = pltpu.VMEM((R * R, 128), F32)
    links = [
        turning,
        turning,
        half,
        half,
        half,
        pltpu.VMEM((nsamp - 1, R // 2, 128), F32),
        pltpu.SemaphoreType.DMA((nsamp - 1,)),
        pltpu.SemaphoreType.DMA((nsamp - 1,)),
        pltpu.SemaphoreType.DMA((2,)),
    ]
    summed = pl.pallas_call(
        functools.partial(gradient_kernel, ncores, nsamp),
        out_shape=(new_slices, square, square),
        in_specs=[vm] * 3 + [pl.BlockSpec(memory_space=pl.ANY), pl.BlockSpec(memory_space=pltpu.SMEM)],
        out_specs=(vm, vm, vm),
        scratch_shapes=[
            pltpu.VMEM((N, R * R), F32),
            pltpu.VMEM((2, parts, nsamp - 1, slab // 2, R * R // parts), F32),
            pltpu.VMEM((N, 128), F32),
            pltpu.VMEM((nsamp - 1, slab, 128), F32),
            pltpu.VMEM((slab, R * R), F32),
            pltpu.SemaphoreType.DMA,
            pltpu.SemaphoreType.DMA((nsamp - 1,)),
            pltpu.SemaphoreType.DMA((nsamp - 1,)),
            pltpu.SemaphoreType.DMA((2, parts, nsamp - 1)),
            pltpu.SemaphoreType.DMA((2, parts, nsamp - 1)),
        ] + links,
        compiler_params=pltpu.CompilerParams(collective_id=2, has_side_effects=True, vmem_limit_bytes=48 << 20),
        name="gradient_sum",
    )
    routed = pl.pallas_call(
        functools.partial(routed_kernel, ncores, nsamp, room),
        out_shape=(new_slices, square, square),
        in_specs=[vm] * 3 + [pl.BlockSpec(memory_space=pl.ANY), pl.BlockSpec(memory_space=pltpu.SMEM)],
        out_specs=(vm, vm, vm),
        scratch_shapes=[
            pltpu.VMEM((nsamp, 2 * R + 8, room), F32),
            pltpu.VMEM((nsamp, 2 * R + 8, room), F32),
            pltpu.VMEM((N, 128), F32),
            pltpu.VMEM((nsamp - 1, slab, 128), F32),
            pltpu.VMEM((slab, R * R), F32),
            pltpu.SemaphoreType.DMA,
            pltpu.SemaphoreType.DMA((nsamp - 1,)),
            pltpu.SemaphoreType.DMA((nsamp - 1,)),
            pltpu.SemaphoreType.DMA((nsamp,)),
            pltpu.SemaphoreType.DMA((nsamp,)),
        ] + links,
        compiler_params=pltpu.CompilerParams(collective_id=3, has_side_effects=True, vmem_limit_bytes=48 << 20),
        name="gradient_routed",
    )
    updated, hprev, hown = lax.cond(over[0, 0] == 0.0, routed, summed,
                       own_index.reshape(1, count), left, right, cores, step_size.reshape(1, 1))
    result = pl.pallas_call(
        finish_kernel,
        out_shape=new_slices,
        in_specs=[vm] * 3,
        out_specs=vm,
        scratch_shapes=[turning, turning],
        compiler_params=pltpu.CompilerParams(vmem_limit_bytes=32 << 20),
        name="finish",
    )(updated, hprev, hown)
    return result[None]


def solution(mesh):
    in_specs = (P("cores", None, None), P("samp", None), P("samp"), P())
    out_specs = P("cores", "samp", None)
    return jax.shard_map(
        on_device, mesh=mesh, in_specs=in_specs, out_specs=out_specs, check_vma=False
    )
```

```python
import functools

import jax
import jax.numpy as jnp
from jax import lax
from jax.experimental import pallas as pl
from jax.experimental.pallas import tpu as pltpu
from jax.sharding import PartitionSpec as P

R = 48
N = 512
W = 64

HIGH = lax.Precision.HIGHEST
MESH = pl.DeviceIdType.MESH
F32 = jnp.float32
BF16 = jnp.bfloat16


def split(x):
    high = x.astype(BF16)
    low = (x - high.astype(F32)).astype(BF16)
    return high, low


def three(x):
    high, low = split(x)
    return jnp.concatenate([high, low, high], axis=0)


def weigh(mat, ustack):
    high, low = split(mat)
    return jnp.dot(jnp.concatenate([high, high, low], axis=1), ustack, preferred_element_type=F32)


def padded(x):
    return jnp.concatenate([x, jnp.zeros((W - x.shape[0], x.shape[1]), F32)], axis=0)


def across(ref, width):
    return jnp.concatenate([ref[pl.ds(n, R, stride=R), :][:, :width] for n in range(R)], axis=1)


def along(ref, width):
    return jnp.concatenate([ref[R * n:R * n + R, :][:, :width] for n in range(R)], axis=1)


def lay(ref, wide, width):
    for n in range(R):
        ref[R * n:R * n + R, 0:width] = wide[:, n * width:n * width + width]


def greet_modes(barrier, nsamp):
    mine = lax.axis_index("cores")

    @pl.when(mine > 0)
    def _():
        for d in range(nsamp):
            pl.semaphore_signal(barrier, inc=1, device_id=(mine - 1, lax.rem(lax.axis_index("samp") + d, nsamp)),
                                device_id_type=MESH)


def chain(ncores, nsamp, slab, turned, hprev, hown, moved, sendbuf, got_prev, got_own,
          send_own, recv_own, send_next, recv_prev):
    mine = lax.axis_index("cores")
    me = lax.axis_index("samp")
    has_prev = mine > 0
    has_next = mine < ncores - 1

    def own_copy(d):
        return pltpu.make_async_remote_copy(
            src_ref=sendbuf, dst_ref=got_own.at[d - 1], send_sem=send_own.at[d - 1],
            recv_sem=recv_own.at[d - 1], device_id=(mine, lax.rem(me + d, nsamp)), device_id_type=MESH)

    def next_copy(d):
        return pltpu.make_async_remote_copy(
            src_ref=sendbuf, dst_ref=got_prev.at[d], send_sem=send_next.at[d], recv_sem=recv_prev.at[d],
            device_id=(lax.rem(mine + 1, ncores), lax.rem(me + d, nsamp)), device_id_type=MESH)

    def take_prev():
        total = jnp.zeros((R // 2, 128), F32)
        for d in range(nsamp):
            next_copy(d).wait_recv()
            total = total + got_prev[d]
        hprev[...] = unpack(total)

    def unpack(x):
        return jnp.concatenate([x[:, :W], x[:, W:]], axis=0)

    row = lax.broadcasted_iota(jnp.int32, (R, W), 0)
    lane = lax.broadcasted_iota(jnp.int32, (R, W), 1)
    eye = (row == lane).astype(F32)
    hprev[...] = eye
    hown[...] = eye

    @pl.when(has_next)
    def _():
        ustack = three(padded(across(turned, slab)))
        zh, zl = split(along(turned, slab))

        @pl.when(has_prev)
        def _():
            take_prev()

        lay(moved, weigh(hprev[...], ustack), slab)
        yh, yl = split(across(moved, slab))
        nt = (((1,), (1,)), ((), ()))
        gram = lax.dot_general(zh, yh, nt, preferred_element_type=F32)
        gram = gram + lax.dot_general(zh, yl, nt, preferred_element_type=F32)
        gram = gram + lax.dot_general(zl, yh, nt, preferred_element_type=F32)
        gram = jnp.concatenate([gram * (1.0 / N), jnp.zeros((R, W - R), F32)], axis=1)
        sendbuf[...] = jnp.concatenate([gram[:R // 2], gram[R // 2:]], axis=1)
        for d in range(nsamp):
            next_copy(d).start()
        for d in range(1, nsamp):
            own_copy(d).start()
        total = sendbuf[...]
        for d in range(1, nsamp):
            own_copy(d).wait_recv()
            total = total + got_own[d - 1]
        hown[...] = unpack(total)
        for d in range(1, nsamp):
            own_copy(d).wait_send()
        for d in range(nsamp):
            next_copy(d).wait_send()

    @pl.when(jnp.logical_not(has_next))
    def _():
        take_prev()


def picker(idx_ref):
    count = idx_ref.shape[1]
    row = lax.broadcasted_iota(jnp.int32, (N, count), 0)
    return jnp.where(row == idx_ref[...], 1.0, 0.0).astype(BF16)


def front_kernel(ncores, nsamp, room, cores, idx, every, observed, left_out, right_out, over, table, mats, sent_l, sent_r, got_l, got_r, pred,
                 flag, got_flag, loads, sems, fsend, frecv):
    mine = lax.axis_index("cores")
    me = lax.axis_index("samp")
    count = idx.shape[1]
    step = 8 * R
    blocks = R // 8
    chunk = 256
    chunks = count // chunk
    first, last = mine == 0, mine == ncores - 1
    inner = jnp.logical_not(jnp.logical_or(first, last))
    barrier = pltpu.get_barrier_semaphore()

    def load(t):
        lanes = pl.ds(pl.multiple_of(t * step, 128), step)
        return pltpu.make_async_copy(cores.at[0, :, lanes], table.at[:, lanes], loads.at[t])

    for t in range(blocks):
        load(t).start()

    @pl.when(mine > 0)
    def _():
        pl.semaphore_signal(barrier, inc=1, device_id=(mine - 1, me), device_id_type=MESH)

    @pl.when(mine < ncores - 1)
    def _():
        pl.semaphore_signal(barrier, inc=1, device_id=(mine + 1, me), device_id_type=MESH)

    for d in range(1, nsamp):
        pl.semaphore_signal(barrier, inc=1, device_id=(mine, lax.rem(me + d, nsamp)), device_id_type=MESH)

    def tell(d):
        return pltpu.make_async_remote_copy(
            src_ref=flag, dst_ref=got_flag.at[d - 1], send_sem=fsend.at[d - 1], recv_sem=frecv.at[d - 1],
            device_id=(mine, lax.rem(me + d, nsamp)), device_id_type=MESH)

    most = jnp.zeros((nsamp, 1), F32)
    owner = lax.broadcasted_iota(jnp.int32, (nsamp, count), 0)
    for m in range(ncores):
        member = jnp.where(every[m:m + 1, :] // (N // nsamp) == owner, 1.0, 0.0)
        most = jnp.maximum(most, jnp.sum(member, axis=1, keepdims=True))
    most = jnp.max(most, axis=0, keepdims=True)
    flag[...] = jnp.broadcast_to(jnp.where(most > room, 1.0, 0.0), (8, 128))

    onehot = picker(idx)
    unit = (lax.broadcasted_iota(jnp.int32, (R, count), 0) == 0).astype(F32)

    def picked(part):
        high, low = split(part.T)
        return (jnp.dot(high, onehot, preferred_element_type=F32)
                + jnp.dot(low, onehot, preferred_element_type=F32))

    @pl.when(first)
    def _():
        load(0).wait()
        sent_l[...] = picked(table[:, 0:128])[0:R]
        got_l[...] = unit
        for t in range(1, blocks):
            load(t).wait()

    @pl.when(last)
    def _():
        for t in range(blocks):
            load(t).wait()
        row = lax.broadcasted_iota(jnp.int32, (R * R, 128), 0)
        col = lax.broadcasted_iota(jnp.int32, (R * R, 128), 1)
        heads = jnp.where(jnp.logical_and(row == col * R, col < R), 1.0, 0.0).astype(BF16)
        high, low = split(table[...])
        part = jnp.dot(high, heads, preferred_element_type=F32) + jnp.dot(low, heads, preferred_element_type=F32)
        sent_r[...] = picked(part)[0:R]
        got_r[...] = unit

    @pl.when(inner)
    def _():
        def fill(t, _):
            load(t).wait()
            at = pl.multiple_of(t * step, step)
            mats[pl.ds(at, step), :] = picked(table[:, pl.ds(at, step)])
            return 0
        lax.fori_loop(0, blocks, fill, 0)

    pl.semaphore_wait(barrier, nsamp - 1 + jnp.minimum(mine, 1) + jnp.minimum(ncores - 1 - mine, 1))
    for d in range(1, nsamp):
        tell(d).start()

    def copy_l(n):
        lanes = pl.ds(n * chunk, chunk)
        return pltpu.make_async_remote_copy(
            src_ref=sent_l.at[:, lanes], dst_ref=got_l.at[:, lanes], send_sem=sems.at[0, n], recv_sem=sems.at[1, n],
            device_id=(lax.rem(mine + 1, ncores), me), device_id_type=MESH)

    def copy_r(n):
        lanes = pl.ds(n * chunk, chunk)
        return pltpu.make_async_remote_copy(
            src_ref=sent_r.at[:, lanes], dst_ref=got_r.at[:, lanes], send_sem=sems.at[2, n], recv_sem=sems.at[3, n],
            device_id=(lax.rem(mine + ncores - 1, ncores), me), device_id_type=MESH)

    def pass_left():
        for n in range(chunks):
            c = n * chunk
            copy_l(n).wait_recv()

            def add(a, total):
                return total + got_l[pl.ds(a, 1), c:c + chunk] * mats[pl.ds(pl.multiple_of(a * R, 8), R), c:c + chunk]
            sent_l[:, c:c + chunk] = lax.fori_loop(0, R, add, jnp.zeros((R, chunk), F32), unroll=4)
            copy_l(n).start()

    def pass_right():
        for n in range(chunks):
            c = n * chunk
            copy_r(n).wait_recv()

            def one(a, _):
                m = mats[pl.ds(pl.multiple_of(a * R, 8), R), c:c + chunk] * got_r[:, c:c + chunk]
                sent_r[pl.ds(a, 1), c:c + chunk] = jnp.sum(m, axis=0, keepdims=True)
                return 0
            lax.fori_loop(0, R, one, 0, unroll=4)
            copy_r(n).start()

    @pl.when(first)
    def _():
        for n in range(chunks):
            copy_l(n).start()
        for n in range(chunks):
            copy_r(n).wait_recv()

    @pl.when(last)
    def _():
        for n in range(chunks):
            copy_r(n).start()
        for n in range(chunks):
            copy_l(n).wait_recv()

    @pl.when(jnp.logical_and(inner, 2 * mine < ncores))
    def _():
        pass_left()
        pass_right()

    @pl.when(jnp.logical_and(inner, 2 * mine >= ncores))
    def _():
        pass_right()
        pass_left()

    @pl.when(last)
    def _():
        pred[...] = jnp.sum(got_l[...] * sent_r[...], axis=0, keepdims=True)

    @pl.when(mine < ncores - 1)
    def _():
        pred[...] = jnp.sum(sent_l[...] * got_r[...], axis=0, keepdims=True)

    left_out[...] = got_l[...]
    right_out[...] = got_r[...] * (pred[...] - observed[...])
    worst = flag[...]
    for d in range(1, nsamp):
        tell(d).wait_recv()
        worst = jnp.maximum(worst, got_flag[d - 1])
    over[...] = worst
    for d in range(1, nsamp):
        tell(d).wait_send()

    @pl.when(mine < ncores - 1)
    def _():
        for n in range(chunks):
            copy_l(n).wait_send()

    @pl.when(mine > 0)
    def _():
        for n in range(chunks):
            copy_r(n).wait_send()


def against(onehot, vecs):
    nt = (((1,), (1,)), ((), ()))
    high, low = split(vecs)
    return (lax.dot_general(onehot, high, nt, preferred_element_type=F32)
            + lax.dot_general(onehot, low, nt, preferred_element_type=F32))


def edge_gradient(nsamp, onehot, left, right, rate, updated, small, got_small, kept, esend, erecv):
    mine = lax.axis_index("cores")
    me = lax.axis_index("samp")
    slab = updated.shape[0]
    at_first = (mine == 0).astype(F32)
    vec = at_first * right[...] + (1.0 - at_first) * left[...] * right[0:1, :]
    pad = jnp.zeros((128 - R, vec.shape[1]), F32)
    small[...] = against(onehot, jnp.concatenate([vec, pad], axis=0))

    def send(d):
        to = lax.rem(me + d, nsamp)
        return pltpu.make_async_remote_copy(
            src_ref=small.at[pl.ds(pl.multiple_of(to * slab, slab), slab)], dst_ref=got_small.at[d - 1],
            send_sem=esend.at[d - 1], recv_sem=erecv.at[d - 1], device_id=(mine, to), device_id_type=MESH)
    for d in range(1, nsamp):
        send(d).start()
    total = small[pl.ds(pl.multiple_of(me * slab, slab), slab), :]
    for d in range(1, nsamp):
        send(d).wait_recv()
        total = total + got_small[d - 1]
    row = lax.broadcasted_iota(jnp.int32, (128, R * R), 0)
    col = lax.broadcasted_iota(jnp.int32, (128, R * R), 1)
    stride = 1 + (R - 1) * jnp.minimum(mine, 1)
    spread = jnp.where(jnp.logical_and(col == row * stride, row < R), 1.0, 0.0).astype(BF16)
    high, low = split(total)
    updated[...] = kept[...] - rate[0, 0] * (jnp.dot(high, spread, preferred_element_type=F32)
                                             + jnp.dot(low, spread, preferred_element_type=F32))
    for d in range(1, nsamp):
        send(d).wait_send()


def gradient_kernel(ncores, nsamp, idx, left, right, cores, rate, turned, hprev, hown, partial, got, small, got_small, kept,
                    ksem, esend, erecv, rsend, rrecv, *links):
    mine = lax.axis_index("cores")
    me = lax.axis_index("samp")
    updated, links = links[0], links[1:]
    slab = updated.shape[0]
    half = slab // 2
    step = 8 * R
    parts = got.shape[1]
    wide = R * R // parts
    edge = jnp.logical_or(mine == 0, mine == ncores - 1)
    inner = jnp.logical_not(edge)
    barrier = pltpu.get_barrier_semaphore()
    for d in range(1, nsamp):
        pl.semaphore_signal(barrier, inc=1, device_id=(mine, lax.rem(me + d, nsamp)), device_id_type=MESH)
    greet_modes(barrier, nsamp)
    keep = pltpu.make_async_copy(cores.at[0, pl.ds(pl.multiple_of(me * slab, slab), slab)], kept, ksem)
    keep.start()
    onehot = picker(idx)
    odd = lax.rem(me, 2)
    place = (1 - odd) * (me // 2) + odd * (nsamp - 1 - me // 2)

    def at_place(p):
        p = lax.rem(p + 2 * nsamp, nsamp)
        up = jnp.minimum(p // (nsamp // 2), 1)
        return (1 - up) * 2 * p + up * (2 * (nsamp - 1 - p) + 1)

    def ring(direction, c, t, peer):
        return pltpu.make_async_remote_copy(
            src_ref=got.at[direction, c, jnp.maximum(t - 1, 0)], dst_ref=got.at[direction, c, t],
            send_sem=rsend.at[direction, c, t], recv_sem=rrecv.at[direction, c, t],
            device_id=(mine, peer), device_id_type=MESH)

    def rows_of(direction, t):
        owner = at_place(place - 1 - t) if direction == 0 else at_place(place + 1 + t)
        return pl.ds(pl.multiple_of(owner * slab + direction * half, half), half)

    up_peer, down_peer = at_place(place + 1), at_place(place - 1)

    def block(t, _):
        lhs = left[pl.ds(pl.multiple_of(t * 8, 8), 8), :]
        outer = jnp.concatenate([lhs[a:a + 1, :] * right[...] for a in range(8)], axis=0)
        partial[:, pl.ds(pl.multiple_of(t * step, 128), step)] = against(onehot, outer)
        return 0

    each = R // 8 // parts

    @pl.when(inner)
    def _():
        lax.fori_loop(0, each, block, 0)

    keep.wait()
    pl.semaphore_wait(barrier, nsamp - 1 + nsamp * jnp.minimum(ncores - 1 - mine, 1))

    @pl.when(inner)
    def _():
        peers = (up_peer, down_peer)

        def begin(c):
            for direction in range(2):
                pltpu.make_async_remote_copy(
                    src_ref=partial.at[rows_of(direction, 0), pl.ds(c * wide, wide)], dst_ref=got.at[direction, c, 0],
                    send_sem=rsend.at[direction, c, 0], recv_sem=rrecv.at[direction, c, 0],
                    device_id=(mine, peers[direction]), device_id_type=MESH).start()

        def hop(c, t):
            for direction in range(2):
                ring(direction, c, t - 1, peers[direction]).wait_recv()
                got[direction, c, t - 1] = (got[direction, c, t - 1]
                                            + partial[rows_of(direction, t), c * wide:c * wide + wide])
                ring(direction, c, t, peers[direction]).start()

        def finish(c):
            end = nsamp - 2
            for direction in range(2):
                ring(direction, c, end, peers[direction]).wait_recv()
                here = (slice(direction * half, direction * half + half), slice(c * wide, c * wide + wide))
                updated[here] = kept[here] - rate[0, 0] * (
                    got[direction, c, end] + partial[rows_of(direction, end + 1), c * wide:c * wide + wide])

        for turn in range(parts):
            if turn > 0:
                lax.fori_loop(turn * each, (turn + 1) * each, block, 0)
            begin(turn)
            for c in range(turn):
                if turn - c <= nsamp - 2:
                    hop(c, turn - c)

        def steady(turn, _):
            for c in range(parts):
                hop(c, turn - c)
            return 0
        lax.fori_loop(parts, nsamp - 1, steady, 0)
        for turn in range(max(parts, nsamp - 1), parts + nsamp - 1):
            for c in range(parts):
                if turn - c <= nsamp - 2:
                    hop(c, turn - c)
                elif turn - c == nsamp - 1:
                    finish(c)

        def drain(t, _):
            for c in range(parts):
                for direction in range(2):
                    ring(direction, c, t, peers[direction]).wait_send()
            return 0
        lax.fori_loop(0, nsamp - 1, drain, 0)

    @pl.when(edge)
    def _():
        edge_gradient(nsamp, onehot, left, right, rate, updated, small, got_small, kept, esend, erecv)

    turned[:, 0:slab] = updated[...].T
    chain(ncores, nsamp, slab, turned, hprev, hown, *links)


def routed_kernel(ncores, nsamp, room, idx, left, right, cores, rate, turned, hprev, hown, packed, got, small, got_small, kept,
                  ksem, esend, erecv, psend, precv, *links):
    mine = lax.axis_index("cores")
    me = lax.axis_index("samp")
    count = idx.shape[1]
    updated, links = links[0], links[1:]
    slab = updated.shape[0]
    edge = jnp.logical_or(mine == 0, mine == ncores - 1)
    barrier = pltpu.get_barrier_semaphore()
    for d in range(1, nsamp):
        pl.semaphore_signal(barrier, inc=1, device_id=(mine, lax.rem(me + d, nsamp)), device_id_type=MESH)
    greet_modes(barrier, nsamp)
    keep = pltpu.make_async_copy(cores.at[0, pl.ds(pl.multiple_of(me * slab, slab), slab)], kept, ksem)
    keep.start()

    @pl.when(edge)
    def _():
        keep.wait()
        pl.semaphore_wait(barrier, nsamp - 1 + nsamp * jnp.minimum(ncores - 1 - mine, 1))
        edge_gradient(nsamp, picker(idx), left, right, rate, updated, small, got_small, kept, esend, erecv)
        turned[:, 0:slab] = updated[...].T

    @pl.when(jnp.logical_not(edge))
    def _():
        slab_of = idx[...] // slab
        member = jnp.where(lax.broadcasted_iota(jnp.int32, (16, count), 0) == slab_of, 1.0, 0.0)
        before = jnp.where(lax.broadcasted_iota(jnp.int32, (count, count), 0)
                           < lax.broadcasted_iota(jnp.int32, (count, count), 1), 1.0, 0.0).astype(BF16)
        earlier = jnp.dot(member.astype(BF16), before, preferred_element_type=F32)
        place = slab_of * room + jnp.sum(member * earlier, axis=0, keepdims=True).astype(jnp.int32)
        high, low = split(jnp.concatenate([left[...], right[...]], axis=0))
        within = jnp.broadcast_to((idx[...] - slab_of * slab).astype(F32), (16, count)).astype(BF16)
        rows = jnp.concatenate([high, low, within], axis=0)
        spot = lax.broadcasted_iota(jnp.int32, (room, count), 0)

        def send(d):
            return pltpu.make_async_remote_copy(
                src_ref=packed.at[d], dst_ref=got.at[d], send_sem=psend.at[d], recv_sem=precv.at[d],
                device_id=(mine, lax.rem(me + d, nsamp)), device_id_type=MESH)

        def pack(d):
            to = lax.rem(me + d, nsamp)
            pick = jnp.where(spot == place - to * room, 1.0, 0.0).astype(BF16)
            out = lax.dot_general(rows, pick, (((1,), (1,)), ((), ())), preferred_element_type=F32)
            return jnp.concatenate([out[:2 * R] + out[2 * R:4 * R], out[4 * R:4 * R + 8]], axis=0)

        def dispatch(d, _):
            packed[d] = pack(d)

            @pl.when(d == 1)
            def _():
                pl.semaphore_wait(barrier, nsamp - 1 + nsamp * jnp.minimum(ncores - 1 - mine, 1))
            send(d).start()
            return 0
        lax.fori_loop(1, nsamp, dispatch, 0)
        got[0] = pack(0)
        keep.wait()
        turned[:, 0:slab] = kept[...].T
        nt = (((1,), (1,)), ((), ()))
        group = count // room
        step = 16 * R
        for g in range(0, nsamp, group):
            for d in range(max(g, 1), g + group):
                send(d).wait_recv()
            vecs = jnp.concatenate([got[d] for d in range(g, g + group)], axis=1)
            ids = vecs[2 * R:2 * R + 1].astype(jnp.int32)
            slices = jnp.where(lax.broadcasted_iota(jnp.int32, (slab, count), 0) == ids, 1.0, 0.0).astype(BF16)
            for t in range(0, R, 16):
                outer = jnp.concatenate([vecs[a:a + 1] * vecs[R:2 * R] for a in range(t, t + 16)], axis=0)
                high, low = split(outer)
                here = slice(t * R, t * R + step)
                turned[here, 0:slab] = turned[here, 0:slab] - rate[0, 0] * (
                    lax.dot_general(high, slices, nt, preferred_element_type=F32)
                    + lax.dot_general(low, slices, nt, preferred_element_type=F32))
        for d in range(1, nsamp):
            send(d).wait_send()

    chain(ncores, nsamp, slab, turned, hprev, hown, *links)


def eliminate(mats):
    row = lax.broadcasted_iota(jnp.int32, (R, 128), 0)
    lane = lax.broadcasted_iota(jnp.int32, (R, 128), 1)
    mats = [jnp.concatenate([m, (row == lane).astype(F32)[:, :W]], axis=1) for m in mats]
    for j in range(0, R, 2):
        nxt = []
        for m in mats:
            col0 = jnp.broadcast_to(m[:, j:j + 1], (R, 128))
            col1 = jnp.broadcast_to(m[:, j + 1:j + 2], (R, 128))
            inv0 = 1.0 / col0[j:j + 1]
            ratio = col0[j + 1:j + 2] * inv0
            inv1 = 1.0 / (col1[j + 1:j + 2] - ratio * col0[j + 1:j + 2])
            row0 = m[j:j + 1]
            row1 = m[j + 1:j + 2] - ratio * row0
            col1 = jnp.where(row > j + 1, col1 - col0 * ratio, 0.0)
            col0 = jnp.where(row > j, col0, 0.0)
            nxt.append(m - col0 * (row0 * inv0) - col1 * (row1 * inv1))
        mats = nxt
    outs = []
    for m in mats:
        diag = jnp.sum(jnp.where(row == lane, m, 0.0), axis=1, keepdims=True)
        outs.append(m * lax.rsqrt(diag))
    return outs


def finish_kernel(turned, hprev, hown, out, last, moved):
    slab = out.shape[0]
    ustack = three(padded(across(turned, slab)))
    first, second = eliminate([hprev[...], hown[...]])
    lay(moved, weigh(first[:, :W], ustack), slab)
    ystack = three(padded(across(moved, slab)))
    lay(last, weigh(second[:, W:], ystack), slab)
    out[...] = last[:, 0:slab].T


def on_device(cores, indices, observed, step_size):
    ncores = lax.axis_size("cores")
    mine = lax.axis_index("cores")
    nsamp = lax.axis_size("samp")
    count = indices.shape[0]
    own_index = lax.dynamic_index_in_dim(indices, mine, 1, keepdims=False)
    slab = N // nsamp
    parts = 3
    room = max(2 * count // nsamp, 128)
    vm = pl.BlockSpec(memory_space=pltpu.VMEM)
    vectors = jax.ShapeDtypeStruct((R, count), F32)
    left, right, over = pl.pallas_call(
        functools.partial(front_kernel, ncores, nsamp, room),
        out_shape=(vectors, vectors, jax.ShapeDtypeStruct((8, 128), F32)),
        in_specs=[pl.BlockSpec(memory_space=pl.ANY), vm, vm, vm],
        out_specs=(vm, vm, vm),
        scratch_shapes=[
            pltpu.VMEM((N, R * R), F32),
            pltpu.VMEM((R * R, count), F32),
            pltpu.VMEM((R, count), F32),
            pltpu.VMEM((R, count), F32),
            pltpu.VMEM((R, count), F32),
            pltpu.VMEM((R, count), F32),
            pltpu.VMEM((1, count), F32),
            pltpu.VMEM((8, 128), F32),
            pltpu.VMEM((nsamp - 1, 8, 128), F32),
            pltpu.SemaphoreType.DMA((R // 8,)),
            pltpu.SemaphoreType.DMA((4, count // 256)),
            pltpu.SemaphoreType.DMA((nsamp - 1,)),
            pltpu.SemaphoreType.DMA((nsamp - 1,)),
        ],
        compiler_params=pltpu.CompilerParams(collective_id=1, has_side_effects=True, vmem_limit_bytes=48 << 20),
        name="sample_vectors",
    )(cores, own_index.reshape(1, count), indices.T, observed.reshape(1, count))
    new_slices = jax.ShapeDtypeStruct((slab, R * R), F32)
    square = jax.ShapeDtypeStruct((R, W), F32)
    turning = pltpu.VMEM((R * R, 128), F32)
    links = [
        pltpu.VMEM((slab, R * R), F32),
        turning,
        pltpu.VMEM((R // 2, 128), F32),
        pltpu.VMEM((nsamp, R // 2, 128), F32),
        pltpu.VMEM((nsamp - 1, R // 2, 128), F32),
        pltpu.SemaphoreType.DMA((nsamp - 1,)),
        pltpu.SemaphoreType.DMA((nsamp - 1,)),
        pltpu.SemaphoreType.DMA((nsamp,)),
        pltpu.SemaphoreType.DMA((nsamp,)),
    ]
    summed = pl.pallas_call(
        functools.partial(gradient_kernel, ncores, nsamp),
        out_shape=(jax.ShapeDtypeStruct((R * R, 128), F32), square, square),
        in_specs=[vm] * 3 + [pl.BlockSpec(memory_space=pl.ANY), pl.BlockSpec(memory_space=pltpu.SMEM)],
        out_specs=(vm, vm, vm),
        scratch_shapes=[
            pltpu.VMEM((N, R * R), F32),
            pltpu.VMEM((2, parts, nsamp - 1, slab // 2, R * R // parts), F32),
            pltpu.VMEM((N, 128), F32),
            pltpu.VMEM((nsamp - 1, slab, 128), F32),
            pltpu.VMEM((slab, R * R), F32),
            pltpu.SemaphoreType.DMA,
            pltpu.SemaphoreType.DMA((nsamp - 1,)),
            pltpu.SemaphoreType.DMA((nsamp - 1,)),
            pltpu.SemaphoreType.DMA((2, parts, nsamp - 1)),
            pltpu.SemaphoreType.DMA((2, parts, nsamp - 1)),
        ] + links,
        compiler_params=pltpu.CompilerParams(collective_id=2, has_side_effects=True, vmem_limit_bytes=48 << 20),
        name="gradient_sum",
    )
    routed = pl.pallas_call(
        functools.partial(routed_kernel, ncores, nsamp, room),
        out_shape=(jax.ShapeDtypeStruct((R * R, 128), F32), square, square),
        in_specs=[vm] * 3 + [pl.BlockSpec(memory_space=pl.ANY), pl.BlockSpec(memory_space=pltpu.SMEM)],
        out_specs=(vm, vm, vm),
        scratch_shapes=[
            pltpu.VMEM((nsamp, 2 * R + 8, room), F32),
            pltpu.VMEM((nsamp, 2 * R + 8, room), F32),
            pltpu.VMEM((N, 128), F32),
            pltpu.VMEM((nsamp - 1, slab, 128), F32),
            pltpu.VMEM((slab, R * R), F32),
            pltpu.SemaphoreType.DMA,
            pltpu.SemaphoreType.DMA((nsamp - 1,)),
            pltpu.SemaphoreType.DMA((nsamp - 1,)),
            pltpu.SemaphoreType.DMA((nsamp,)),
            pltpu.SemaphoreType.DMA((nsamp,)),
        ] + links,
        compiler_params=pltpu.CompilerParams(collective_id=3, has_side_effects=True, vmem_limit_bytes=48 << 20),
        name="gradient_routed",
    )
    updated, hprev, hown = lax.cond(over[0, 0] == 0.0, routed, summed,
                       own_index.reshape(1, count), left, right, cores, step_size.reshape(1, 1))
    result = pl.pallas_call(
        finish_kernel,
        out_shape=new_slices,
        in_specs=[vm] * 3,
        out_specs=vm,
        scratch_shapes=[turning, turning],
        compiler_params=pltpu.CompilerParams(vmem_limit_bytes=32 << 20),
        name="finish",
    )(updated, hprev, hown)
    return result[None]


def solution(mesh):
    in_specs = (P("cores", None, None), P("samp", None), P("samp"), P())
    out_specs = P("cores", "samp", None)
    return jax.shard_map(
        on_device, mesh=mesh, in_specs=in_specs, out_specs=out_specs, check_vma=False
    )
```

```python
import functools

import jax
import jax.numpy as jnp
from jax import lax
from jax.experimental import pallas as pl
from jax.experimental.pallas import tpu as pltpu
from jax.sharding import PartitionSpec as P

R = 48
N = 512
W = 64

HIGH = lax.Precision.HIGHEST
MESH = pl.DeviceIdType.MESH
F32 = jnp.float32
BF16 = jnp.bfloat16


def split(x):
    high = x.astype(BF16)
    low = (x - high.astype(F32)).astype(BF16)
    return high, low


def three(x):
    high, low = split(x)
    return jnp.concatenate([high, low, high], axis=0)


def weigh(mat, ustack):
    high, low = split(mat)
    return jnp.dot(jnp.concatenate([high, high, low], axis=1), ustack, preferred_element_type=F32)


def padded(x):
    return jnp.concatenate([x, jnp.zeros((W - x.shape[0], x.shape[1]), F32)], axis=0)


def across(ref, width):
    return jnp.concatenate([ref[pl.ds(n, R, stride=R), :][:, :width] for n in range(R)], axis=1)


def along(ref, width):
    return jnp.concatenate([ref[R * n:R * n + R, :][:, :width] for n in range(R)], axis=1)


def lay(ref, wide, width):
    for n in range(R):
        ref[R * n:R * n + R, 0:width] = wide[:, n * width:n * width + width]


def greet_modes(barrier, nsamp):
    mine = lax.axis_index("cores")

    @pl.when(mine > 0)
    def _():
        for d in range(nsamp):
            pl.semaphore_signal(barrier, inc=1, device_id=(mine - 1, lax.rem(lax.axis_index("samp") + d, nsamp)),
                                device_id_type=MESH)


def chain(ncores, nsamp, slab, turned, hprev, hown, moved, sendbuf, got_prev, got_own,
          send_own, recv_own, send_next, recv_prev):
    mine = lax.axis_index("cores")
    me = lax.axis_index("samp")
    has_prev = mine > 0
    has_next = mine < ncores - 1

    def own_copy(d):
        return pltpu.make_async_remote_copy(
            src_ref=sendbuf, dst_ref=got_own.at[d - 1], send_sem=send_own.at[d - 1],
            recv_sem=recv_own.at[d - 1], device_id=(mine, lax.rem(me + d, nsamp)), device_id_type=MESH)

    def next_copy(d):
        return pltpu.make_async_remote_copy(
            src_ref=sendbuf, dst_ref=got_prev.at[d], send_sem=send_next.at[d], recv_sem=recv_prev.at[d],
            device_id=(lax.rem(mine + 1, ncores), lax.rem(me + d, nsamp)), device_id_type=MESH)

    def take_prev():
        total = jnp.zeros((R // 2, 128), F32)
        for d in range(nsamp):
            next_copy(d).wait_recv()
            total = total + got_prev[d]
        hprev[...] = unpack(total)

    def unpack(x):
        return jnp.concatenate([x[:, :W], x[:, W:]], axis=0)

    row = lax.broadcasted_iota(jnp.int32, (R, W), 0)
    lane = lax.broadcasted_iota(jnp.int32, (R, W), 1)
    eye = (row == lane).astype(F32)
    hprev[...] = eye
    hown[...] = eye

    @pl.when(has_next)
    def _():
        ustack = three(padded(across(turned, slab)))
        zh, zl = split(along(turned, slab))

        @pl.when(has_prev)
        def _():
            take_prev()

        lay(moved, weigh(hprev[...], ustack), slab)
        yh, yl = split(across(moved, slab))
        nt = (((1,), (1,)), ((), ()))
        gram = lax.dot_general(jnp.concatenate([zh, zl], axis=0), yh, nt, preferred_element_type=F32)
        gram = gram[:R] + gram[R:] + lax.dot_general(zh, yl, nt, preferred_element_type=F32)
        gram = jnp.concatenate([gram * (1.0 / N), jnp.zeros((R, W - R), F32)], axis=1)
        sendbuf[...] = jnp.concatenate([gram[:R // 2], gram[R // 2:]], axis=1)
        for d in range(nsamp):
            next_copy(d).start()
        for d in range(1, nsamp):
            own_copy(d).start()
        total = sendbuf[...]
        for d in range(1, nsamp):
            own_copy(d).wait_recv()
            total = total + got_own[d - 1]
        hown[...] = unpack(total)
        for d in range(1, nsamp):
            own_copy(d).wait_send()
        for d in range(nsamp):
            next_copy(d).wait_send()

    @pl.when(jnp.logical_not(has_next))
    def _():
        take_prev()


def picker(idx_ref):
    count = idx_ref.shape[1]
    row = lax.broadcasted_iota(jnp.int32, (N, count), 0)
    return jnp.where(row == idx_ref[...], 1.0, 0.0).astype(BF16)


def front_kernel(ncores, nsamp, room, cores, idx, every, observed, left_out, right_out, over, table, mats, sent_l, sent_r, got_l, got_r, pred,
                 flag, got_flag, loads, sems, fsend, frecv):
    mine = lax.axis_index("cores")
    me = lax.axis_index("samp")
    count = idx.shape[1]
    step = 8 * R
    blocks = R // 8
    chunk = 256
    chunks = count // chunk
    first, last = mine == 0, mine == ncores - 1
    inner = jnp.logical_not(jnp.logical_or(first, last))
    barrier = pltpu.get_barrier_semaphore()

    def load(t):
        lanes = pl.ds(pl.multiple_of(t * step, 128), step)
        return pltpu.make_async_copy(cores.at[0, :, lanes], table.at[:, lanes], loads.at[t])

    for t in range(blocks):
        load(t).start()

    @pl.when(mine > 0)
    def _():
        pl.semaphore_signal(barrier, inc=1, device_id=(mine - 1, me), device_id_type=MESH)

    @pl.when(mine < ncores - 1)
    def _():
        pl.semaphore_signal(barrier, inc=1, device_id=(mine + 1, me), device_id_type=MESH)

    for d in range(1, nsamp):
        pl.semaphore_signal(barrier, inc=1, device_id=(mine, lax.rem(me + d, nsamp)), device_id_type=MESH)

    def tell(d):
        return pltpu.make_async_remote_copy(
            src_ref=flag, dst_ref=got_flag.at[d - 1], send_sem=fsend.at[d - 1], recv_sem=frecv.at[d - 1],
            device_id=(mine, lax.rem(me + d, nsamp)), device_id_type=MESH)

    most = jnp.zeros((nsamp, 1), F32)
    owner = lax.broadcasted_iota(jnp.int32, (nsamp, count), 0)
    for m in range(ncores):
        member = jnp.where(every[m:m + 1, :] // (N // nsamp) == owner, 1.0, 0.0)
        most = jnp.maximum(most, jnp.sum(member, axis=1, keepdims=True))
    most = jnp.max(most, axis=0, keepdims=True)
    flag[...] = jnp.broadcast_to(jnp.where(most > room, 1.0, 0.0), (8, 128))

    onehot = picker(idx)
    unit = (lax.broadcasted_iota(jnp.int32, (R, count), 0) == 0).astype(F32)

    def picked(part):
        out = jnp.dot(jnp.concatenate(split(part.T), axis=0), onehot, preferred_element_type=F32)
        return out[:part.shape[1]] + out[part.shape[1]:]

    @pl.when(first)
    def _():
        load(0).wait()
        sent_l[...] = picked(table[:, 0:128])[0:R]
        got_l[...] = unit
        for t in range(1, blocks):
            load(t).wait()

    @pl.when(last)
    def _():
        for t in range(blocks):
            load(t).wait()
        row = lax.broadcasted_iota(jnp.int32, (R * R, 128), 0)
        col = lax.broadcasted_iota(jnp.int32, (R * R, 128), 1)
        heads = jnp.where(jnp.logical_and(row == col * R, col < R), 1.0, 0.0).astype(BF16)
        high, low = split(table[...])
        part = jnp.dot(high, heads, preferred_element_type=F32) + jnp.dot(low, heads, preferred_element_type=F32)
        sent_r[...] = picked(part)[0:R]
        got_r[...] = unit

    @pl.when(inner)
    def _():
        def fill(t, _):
            load(t).wait()
            at = pl.multiple_of(t * step, step)
            mats[pl.ds(at, step), :] = picked(table[:, pl.ds(at, step)])
            return 0
        lax.fori_loop(0, blocks, fill, 0)

    pl.semaphore_wait(barrier, nsamp - 1 + jnp.minimum(mine, 1) + jnp.minimum(ncores - 1 - mine, 1))
    for d in range(1, nsamp):
        tell(d).start()

    def copy_l(n):
        lanes = pl.ds(n * chunk, chunk)
        return pltpu.make_async_remote_copy(
            src_ref=sent_l.at[:, lanes], dst_ref=got_l.at[:, lanes], send_sem=sems.at[0, n], recv_sem=sems.at[1, n],
            device_id=(lax.rem(mine + 1, ncores), me), device_id_type=MESH)

    def copy_r(n):
        lanes = pl.ds(n * chunk, chunk)
        return pltpu.make_async_remote_copy(
            src_ref=sent_r.at[:, lanes], dst_ref=got_r.at[:, lanes], send_sem=sems.at[2, n], recv_sem=sems.at[3, n],
            device_id=(lax.rem(mine + ncores - 1, ncores), me), device_id_type=MESH)

    def pass_left():
        for n in range(chunks):
            c = n * chunk
            copy_l(n).wait_recv()

            def add(a, total):
                return total + got_l[pl.ds(a, 1), c:c + chunk] * mats[pl.ds(pl.multiple_of(a * R, 8), R), c:c + chunk]
            sent_l[:, c:c + chunk] = lax.fori_loop(0, R, add, jnp.zeros((R, chunk), F32), unroll=4)
            copy_l(n).start()

    def pass_right():
        for n in range(chunks):
            c = n * chunk
            copy_r(n).wait_recv()

            def one(a, _):
                m = mats[pl.ds(pl.multiple_of(a * R, 8), R), c:c + chunk] * got_r[:, c:c + chunk]
                sent_r[pl.ds(a, 1), c:c + chunk] = jnp.sum(m, axis=0, keepdims=True)
                return 0
            lax.fori_loop(0, R, one, 0, unroll=4)
            copy_r(n).start()

    @pl.when(first)
    def _():
        for n in range(chunks):
            copy_l(n).start()
        for n in range(chunks):
            copy_r(n).wait_recv()

    @pl.when(last)
    def _():
        for n in range(chunks):
            copy_r(n).start()
        for n in range(chunks):
            copy_l(n).wait_recv()

    @pl.when(jnp.logical_and(inner, 2 * mine < ncores))
    def _():
        pass_left()
        pass_right()

    @pl.when(jnp.logical_and(inner, 2 * mine >= ncores))
    def _():
        pass_right()
        pass_left()

    @pl.when(last)
    def _():
        pred[...] = jnp.sum(got_l[...] * sent_r[...], axis=0, keepdims=True)

    @pl.when(mine < ncores - 1)
    def _():
        pred[...] = jnp.sum(sent_l[...] * got_r[...], axis=0, keepdims=True)

    left_out[...] = got_l[...]
    right_out[...] = got_r[...] * (pred[...] - observed[...])
    worst = flag[...]
    for d in range(1, nsamp):
        tell(d).wait_recv()
        worst = jnp.maximum(worst, got_flag[d - 1])
    over[...] = worst
    for d in range(1, nsamp):
        tell(d).wait_send()

    @pl.when(mine < ncores - 1)
    def _():
        for n in range(chunks):
            copy_l(n).wait_send()

    @pl.when(mine > 0)
    def _():
        for n in range(chunks):
            copy_r(n).wait_send()


def against(onehot, vecs):
    nt = (((1,), (1,)), ((), ()))
    high, low = split(vecs)
    return (lax.dot_general(onehot, high, nt, preferred_element_type=F32)
            + lax.dot_general(onehot, low, nt, preferred_element_type=F32))


def edge_gradient(nsamp, onehot, left, right, rate, updated, small, got_small, kept, esend, erecv):
    mine = lax.axis_index("cores")
    me = lax.axis_index("samp")
    slab = updated.shape[0]
    at_first = (mine == 0).astype(F32)
    vec = at_first * right[...] + (1.0 - at_first) * left[...] * right[0:1, :]
    pad = jnp.zeros((128 - R, vec.shape[1]), F32)
    small[...] = against(onehot, jnp.concatenate([vec, pad], axis=0))

    def send(d):
        to = lax.rem(me + d, nsamp)
        return pltpu.make_async_remote_copy(
            src_ref=small.at[pl.ds(pl.multiple_of(to * slab, slab), slab)], dst_ref=got_small.at[d - 1],
            send_sem=esend.at[d - 1], recv_sem=erecv.at[d - 1], device_id=(mine, to), device_id_type=MESH)
    for d in range(1, nsamp):
        send(d).start()
    total = small[pl.ds(pl.multiple_of(me * slab, slab), slab), :]
    for d in range(1, nsamp):
        send(d).wait_recv()
        total = total + got_small[d - 1]
    row = lax.broadcasted_iota(jnp.int32, (128, R * R), 0)
    col = lax.broadcasted_iota(jnp.int32, (128, R * R), 1)
    stride = 1 + (R - 1) * jnp.minimum(mine, 1)
    spread = jnp.where(jnp.logical_and(col == row * stride, row < R), 1.0, 0.0).astype(BF16)
    high, low = split(total)
    updated[...] = kept[...] - rate[0, 0] * (jnp.dot(high, spread, preferred_element_type=F32)
                                             + jnp.dot(low, spread, preferred_element_type=F32))
    for d in range(1, nsamp):
        send(d).wait_send()


def gradient_kernel(ncores, nsamp, idx, left, right, cores, rate, turned, hprev, hown, partial, got, small, got_small, kept,
                    ksem, esend, erecv, rsend, rrecv, *links):
    mine = lax.axis_index("cores")
    me = lax.axis_index("samp")
    updated, links = links[0], links[1:]
    slab = updated.shape[0]
    half = slab // 2
    step = 8 * R
    parts = got.shape[1]
    wide = R * R // parts
    edge = jnp.logical_or(mine == 0, mine == ncores - 1)
    inner = jnp.logical_not(edge)
    barrier = pltpu.get_barrier_semaphore()
    for d in range(1, nsamp):
        pl.semaphore_signal(barrier, inc=1, device_id=(mine, lax.rem(me + d, nsamp)), device_id_type=MESH)
    greet_modes(barrier, nsamp)
    keep = pltpu.make_async_copy(cores.at[0, pl.ds(pl.multiple_of(me * slab, slab), slab)], kept, ksem)
    keep.start()
    onehot = picker(idx)
    odd = lax.rem(me, 2)
    place = (1 - odd) * (me // 2) + odd * (nsamp - 1 - me // 2)

    def at_place(p):
        p = lax.rem(p + 2 * nsamp, nsamp)
        up = jnp.minimum(p // (nsamp // 2), 1)
        return (1 - up) * 2 * p + up * (2 * (nsamp - 1 - p) + 1)

    def ring(direction, c, t, peer):
        return pltpu.make_async_remote_copy(
            src_ref=got.at[direction, c, jnp.maximum(t - 1, 0)], dst_ref=got.at[direction, c, t],
            send_sem=rsend.at[direction, c, t], recv_sem=rrecv.at[direction, c, t],
            device_id=(mine, peer), device_id_type=MESH)

    def rows_of(direction, t):
        owner = at_place(place - 1 - t) if direction == 0 else at_place(place + 1 + t)
        return pl.ds(pl.multiple_of(owner * slab + direction * half, half), half)

    up_peer, down_peer = at_place(place + 1), at_place(place - 1)

    def block(t, _):
        lhs = left[pl.ds(pl.multiple_of(t * 8, 8), 8), :]
        outer = jnp.concatenate([lhs[a:a + 1, :] * right[...] for a in range(8)], axis=0)
        partial[:, pl.ds(pl.multiple_of(t * step, 128), step)] = against(onehot, outer)
        return 0

    each = R // 8 // parts

    @pl.when(inner)
    def _():
        lax.fori_loop(0, each, block, 0)

    keep.wait()
    pl.semaphore_wait(barrier, nsamp - 1 + nsamp * jnp.minimum(ncores - 1 - mine, 1))

    @pl.when(inner)
    def _():
        peers = (up_peer, down_peer)

        def begin(c):
            for direction in range(2):
                pltpu.make_async_remote_copy(
                    src_ref=partial.at[rows_of(direction, 0), pl.ds(c * wide, wide)], dst_ref=got.at[direction, c, 0],
                    send_sem=rsend.at[direction, c, 0], recv_sem=rrecv.at[direction, c, 0],
                    device_id=(mine, peers[direction]), device_id_type=MESH).start()

        def hop(c, t):
            for direction in range(2):
                ring(direction, c, t - 1, peers[direction]).wait_recv()
                got[direction, c, t - 1] = (got[direction, c, t - 1]
                                            + partial[rows_of(direction, t), c * wide:c * wide + wide])
                ring(direction, c, t, peers[direction]).start()

        def finish(c):
            end = nsamp - 2
            for direction in range(2):
                ring(direction, c, end, peers[direction]).wait_recv()
                here = (slice(direction * half, direction * half + half), slice(c * wide, c * wide + wide))
                updated[here] = kept[here] - rate[0, 0] * (
                    got[direction, c, end] + partial[rows_of(direction, end + 1), c * wide:c * wide + wide])

        for turn in range(parts):
            if turn > 0:
                lax.fori_loop(turn * each, (turn + 1) * each, block, 0)
            begin(turn)
            for c in range(turn):
                if turn - c <= nsamp - 2:
                    hop(c, turn - c)

        def steady(turn, _):
            for c in range(parts):
                hop(c, turn - c)
            return 0
        lax.fori_loop(parts, nsamp - 1, steady, 0)
        for turn in range(max(parts, nsamp - 1), parts + nsamp - 1):
            for c in range(parts):
                if turn - c <= nsamp - 2:
                    hop(c, turn - c)
                elif turn - c == nsamp - 1:
                    finish(c)

        def drain(t, _):
            for c in range(parts):
                for direction in range(2):
                    ring(direction, c, t, peers[direction]).wait_send()
            return 0
        lax.fori_loop(0, nsamp - 1, drain, 0)

    @pl.when(edge)
    def _():
        edge_gradient(nsamp, onehot, left, right, rate, updated, small, got_small, kept, esend, erecv)

    turned[:, 0:slab] = updated[...].T
    chain(ncores, nsamp, slab, turned, hprev, hown, *links)


def routed_kernel(ncores, nsamp, room, idx, left, right, cores, rate, turned, hprev, hown, packed, got, small, got_small, kept,
                  ksem, esend, erecv, psend, precv, *links):
    mine = lax.axis_index("cores")
    me = lax.axis_index("samp")
    count = idx.shape[1]
    updated, links = links[0], links[1:]
    slab = updated.shape[0]
    edge = jnp.logical_or(mine == 0, mine == ncores - 1)
    barrier = pltpu.get_barrier_semaphore()
    for d in range(1, nsamp):
        pl.semaphore_signal(barrier, inc=1, device_id=(mine, lax.rem(me + d, nsamp)), device_id_type=MESH)
    greet_modes(barrier, nsamp)
    keep = pltpu.make_async_copy(cores.at[0, pl.ds(pl.multiple_of(me * slab, slab), slab)], kept, ksem)
    keep.start()

    @pl.when(edge)
    def _():
        keep.wait()
        pl.semaphore_wait(barrier, nsamp - 1 + nsamp * jnp.minimum(ncores - 1 - mine, 1))
        edge_gradient(nsamp, picker(idx), left, right, rate, updated, small, got_small, kept, esend, erecv)
        turned[:, 0:slab] = updated[...].T

    @pl.when(jnp.logical_not(edge))
    def _():
        slab_of = idx[...] // slab
        member = jnp.where(lax.broadcasted_iota(jnp.int32, (16, count), 0) == slab_of, 1.0, 0.0)
        before = jnp.where(lax.broadcasted_iota(jnp.int32, (count, count), 0)
                           < lax.broadcasted_iota(jnp.int32, (count, count), 1), 1.0, 0.0).astype(BF16)
        earlier = jnp.dot(member.astype(BF16), before, preferred_element_type=F32)
        place = slab_of * room + jnp.sum(member * earlier, axis=0, keepdims=True).astype(jnp.int32)
        high, low = split(jnp.concatenate([left[...], right[...]], axis=0))
        within = jnp.broadcast_to((idx[...] - slab_of * slab).astype(F32), (16, count)).astype(BF16)
        rows = jnp.concatenate([high, low, within], axis=0)
        spot = lax.broadcasted_iota(jnp.int32, (room, count), 0)

        def send(d):
            return pltpu.make_async_remote_copy(
                src_ref=packed.at[d], dst_ref=got.at[d], send_sem=psend.at[d], recv_sem=precv.at[d],
                device_id=(mine, lax.rem(me + d, nsamp)), device_id_type=MESH)

        def pack(d):
            to = lax.rem(me + d, nsamp)
            pick = jnp.where(spot == place - to * room, 1.0, 0.0).astype(BF16)
            out = lax.dot_general(rows, pick, (((1,), (1,)), ((), ())), preferred_element_type=F32)
            return jnp.concatenate([out[:2 * R] + out[2 * R:4 * R], out[4 * R:4 * R + 8]], axis=0)

        def dispatch(d, _):
            packed[d] = pack(d)

            @pl.when(d == 1)
            def _():
                pl.semaphore_wait(barrier, nsamp - 1 + nsamp * jnp.minimum(ncores - 1 - mine, 1))
            send(d).start()
            return 0
        lax.fori_loop(1, nsamp, dispatch, 0)
        got[0] = pack(0)
        keep.wait()
        turned[:, 0:slab] = kept[...].T
        nt = (((1,), (1,)), ((), ()))
        group = count // room
        step = 16 * R
        for g in range(0, nsamp, group):
            for d in range(max(g, 1), g + group):
                send(d).wait_recv()
            vecs = jnp.concatenate([got[d] for d in range(g, g + group)], axis=1)
            ids = vecs[2 * R:2 * R + 1].astype(jnp.int32)
            slices = jnp.where(lax.broadcasted_iota(jnp.int32, (slab, count), 0) == ids, 1.0, 0.0).astype(BF16)
            for t in range(0, R, 16):
                outer = jnp.concatenate([vecs[a:a + 1] * vecs[R:2 * R] for a in range(t, t + 16)], axis=0)
                out = lax.dot_general(jnp.concatenate(split(outer), axis=0), slices, nt, preferred_element_type=F32)
                here = slice(t * R, t * R + step)
                turned[here, 0:slab] = turned[here, 0:slab] - rate[0, 0] * (out[:step] + out[step:])
        for d in range(1, nsamp):
            send(d).wait_send()

    chain(ncores, nsamp, slab, turned, hprev, hown, *links)


def eliminate(mats):
    row = lax.broadcasted_iota(jnp.int32, (R, 128), 0)
    lane = lax.broadcasted_iota(jnp.int32, (R, 128), 1)
    mats = [jnp.concatenate([m, (row == lane).astype(F32)[:, :W]], axis=1) for m in mats]
    for j in range(0, R, 2):
        nxt = []
        for m in mats:
            col0 = jnp.broadcast_to(m[:, j:j + 1], (R, 128))
            col1 = jnp.broadcast_to(m[:, j + 1:j + 2], (R, 128))
            inv0 = 1.0 / col0[j:j + 1]
            ratio = col0[j + 1:j + 2] * inv0
            inv1 = 1.0 / (col1[j + 1:j + 2] - ratio * col0[j + 1:j + 2])
            row0 = m[j:j + 1]
            row1 = m[j + 1:j + 2] - ratio * row0
            col1 = jnp.where(row > j + 1, col1 - col0 * ratio, 0.0)
            col0 = jnp.where(row > j, col0, 0.0)
            nxt.append(m - col0 * (row0 * inv0) - col1 * (row1 * inv1))
        mats = nxt
    outs = []
    for m in mats:
        diag = jnp.sum(jnp.where(row == lane, m, 0.0), axis=1, keepdims=True)
        outs.append(m * lax.rsqrt(diag))
    return outs


def finish_kernel(turned, hprev, hown, out, last, moved):
    slab = out.shape[0]
    ustack = three(padded(across(turned, slab)))
    first, second = eliminate([hprev[...], hown[...]])
    lay(moved, weigh(first[:, :W], ustack), slab)
    ystack = three(padded(across(moved, slab)))
    lay(last, weigh(second[:, W:], ystack), slab)
    out[...] = last[:, 0:slab].T


def on_device(cores, indices, observed, step_size):
    ncores = lax.axis_size("cores")
    mine = lax.axis_index("cores")
    nsamp = lax.axis_size("samp")
    count = indices.shape[0]
    own_index = lax.dynamic_index_in_dim(indices, mine, 1, keepdims=False)
    slab = N // nsamp
    parts = 3
    room = max(2 * count // nsamp, 128)
    vm = pl.BlockSpec(memory_space=pltpu.VMEM)
    vectors = jax.ShapeDtypeStruct((R, count), F32)
    left, right, over = pl.pallas_call(
        functools.partial(front_kernel, ncores, nsamp, room),
        out_shape=(vectors, vectors, jax.ShapeDtypeStruct((8, 128), F32)),
        in_specs=[pl.BlockSpec(memory_space=pl.ANY), vm, vm, vm],
        out_specs=(vm, vm, vm),
        scratch_shapes=[
            pltpu.VMEM((N, R * R), F32),
            pltpu.VMEM((R * R, count), F32),
            pltpu.VMEM((R, count), F32),
            pltpu.VMEM((R, count), F32),
            pltpu.VMEM((R, count), F32),
            pltpu.VMEM((R, count), F32),
            pltpu.VMEM((1, count), F32),
            pltpu.VMEM((8, 128), F32),
            pltpu.VMEM((nsamp - 1, 8, 128), F32),
            pltpu.SemaphoreType.DMA((R // 8,)),
            pltpu.SemaphoreType.DMA((4, count // 256)),
            pltpu.SemaphoreType.DMA((nsamp - 1,)),
            pltpu.SemaphoreType.DMA((nsamp - 1,)),
        ],
        compiler_params=pltpu.CompilerParams(collective_id=1, has_side_effects=True, vmem_limit_bytes=48 << 20),
        name="sample_vectors",
    )(cores, own_index.reshape(1, count), indices.T, observed.reshape(1, count))
    new_slices = jax.ShapeDtypeStruct((slab, R * R), F32)
    square = jax.ShapeDtypeStruct((R, W), F32)
    turning = pltpu.VMEM((R * R, 128), F32)
    links = [
        pltpu.VMEM((slab, R * R), F32),
        turning,
        pltpu.VMEM((R // 2, 128), F32),
        pltpu.VMEM((nsamp, R // 2, 128), F32),
        pltpu.VMEM((nsamp - 1, R // 2, 128), F32),
        pltpu.SemaphoreType.DMA((nsamp - 1,)),
        pltpu.SemaphoreType.DMA((nsamp - 1,)),
        pltpu.SemaphoreType.DMA((nsamp,)),
        pltpu.SemaphoreType.DMA((nsamp,)),
    ]
    summed = pl.pallas_call(
        functools.partial(gradient_kernel, ncores, nsamp),
        out_shape=(jax.ShapeDtypeStruct((R * R, 128), F32), square, square),
        in_specs=[vm] * 3 + [pl.BlockSpec(memory_space=pl.ANY), pl.BlockSpec(memory_space=pltpu.SMEM)],
        out_specs=(vm, vm, vm),
        scratch_shapes=[
            pltpu.VMEM((N, R * R), F32),
            pltpu.VMEM((2, parts, nsamp - 1, slab // 2, R * R // parts), F32),
            pltpu.VMEM((N, 128), F32),
            pltpu.VMEM((nsamp - 1, slab, 128), F32),
            pltpu.VMEM((slab, R * R), F32),
            pltpu.SemaphoreType.DMA,
            pltpu.SemaphoreType.DMA((nsamp - 1,)),
            pltpu.SemaphoreType.DMA((nsamp - 1,)),
            pltpu.SemaphoreType.DMA((2, parts, nsamp - 1)),
            pltpu.SemaphoreType.DMA((2, parts, nsamp - 1)),
        ] + links,
        compiler_params=pltpu.CompilerParams(collective_id=2, has_side_effects=True, vmem_limit_bytes=48 << 20),
        name="gradient_sum",
    )
    routed = pl.pallas_call(
        functools.partial(routed_kernel, ncores, nsamp, room),
        out_shape=(jax.ShapeDtypeStruct((R * R, 128), F32), square, square),
        in_specs=[vm] * 3 + [pl.BlockSpec(memory_space=pl.ANY), pl.BlockSpec(memory_space=pltpu.SMEM)],
        out_specs=(vm, vm, vm),
        scratch_shapes=[
            pltpu.VMEM((nsamp, 2 * R + 8, room), F32),
            pltpu.VMEM((nsamp, 2 * R + 8, room), F32),
            pltpu.VMEM((N, 128), F32),
            pltpu.VMEM((nsamp - 1, slab, 128), F32),
            pltpu.VMEM((slab, R * R), F32),
            pltpu.SemaphoreType.DMA,
            pltpu.SemaphoreType.DMA((nsamp - 1,)),
            pltpu.SemaphoreType.DMA((nsamp - 1,)),
            pltpu.SemaphoreType.DMA((nsamp,)),
            pltpu.SemaphoreType.DMA((nsamp,)),
        ] + links,
        compiler_params=pltpu.CompilerParams(collective_id=3, has_side_effects=True, vmem_limit_bytes=48 << 20),
        name="gradient_routed",
    )
    updated, hprev, hown = lax.cond(over[0, 0] == 0.0, routed, summed,
                       own_index.reshape(1, count), left, right, cores, step_size.reshape(1, 1))
    result = pl.pallas_call(
        finish_kernel,
        out_shape=new_slices,
        in_specs=[vm] * 3,
        out_specs=vm,
        scratch_shapes=[turning, turning],
        compiler_params=pltpu.CompilerParams(vmem_limit_bytes=32 << 20),
        name="finish",
    )(updated, hprev, hown)
    return result[None]


def solution(mesh):
    in_specs = (P("cores", None, None), P("samp", None), P("samp"), P())
    out_specs = P("cores", "samp", None)
    return jax.shard_map(
        on_device, mesh=mesh, in_specs=in_specs, out_specs=out_specs, check_vma=False
    )
```
